512 devices in a mesh: dp: 32 (over y, z_lo, core), cent: 16 (over x, z_hi).
Axes of the slice: x: 4, y: 8, z: 8 (z_hi: 4, z_lo: 2; z = z_hi * 2 + z_lo), core: 2. Of those that a mesh axis runs over, the one named last changes fastest.
Arguments:
- points: bfloat16 [131072, 1024], P(('dp', 'cent')), may hold values from -6 to 6
- owner_block: int32 [131072, 1], P(('dp', 'cent')), may hold values from 0 to 15; in each aligned block of 256 rows (0 to 255, 256 to 511, ...) at most 32 rows name the same one
- centroid_slot: int32 [131072], P(('dp', 'cent')), may hold values from 0 to 127
- old_first: bfloat16 [2048, 1024], P(('dp', 'cent')), may hold values from -6 to 6
- group_second: int32 [2048], P(('dp', 'cent')), may hold values from 0 to 255
- group_third: int32 [256], replicated, may hold values from 0 to 15
- old_second: bfloat16 [256, 1024], replicated, may hold values from -6 to 6
- old_third: bfloat16 [16, 1024], replicated, may hold values from -6 to 6
Outputs:
- first_centroids: bfloat16 [2048, 1024], P(('dp', 'cent'))
- second_centroids: bfloat16 [256, 1024], replicated
- third_centroids: bfloat16 [16, 1024], replicated
- best_scores: float32 [131072], P(('dp', 'cent'))
The draws below stay inside these ranges and needn't reach their ends.
Inputs may be any that keep to these rules, and one draw needn't show every extreme that they name: `owner_block`: in the rows of one device at most 32 points name one owner block, and some owner block is named by exactly 32 of them.
All inputs are finite; a program needn't handle non-finite values.
Results may differ from the reference program's by a relative error of at most 0.0012.
Values may be sent and summed in bfloat16 or wider, within the bound.
A program may use at most 64 MiB of HBM per device.

```python
import math
import jax
import jax.numpy as jnp
import numpy as np
from jax import lax

D = 1024
P_DEV = 256
K1_CENT = 128
K2 = 256
K3 = 16
BLOCKS = 16
R1 = 4
CAP = 32
K1 = 2048
POINTS = 131072


def set_ends(array, own_key, smallest, top_value):
    shape = array.shape
    spot = [jax.random.randint(jax.random.fold_in(own_key, axis), (), 0, shape[axis]) for axis in range(len(shape))]
    array = array.at[tuple(spot)].set(smallest)
    longest = shape.index(max(shape))
    spot[longest] = (spot[longest] + 1) % shape[longest]
    return array.at[tuple(spot)].set(top_value)


def steps_of(rng, dims, cuts, least, top_value):
    def one(position, parts):
        heights = jax.random.uniform(jax.random.fold_in(jax.random.fold_in(rng, 6), position), (parts,), jnp.float32, least / len(cuts), top_value / len(cuts))
        return jnp.repeat(jnp.exp(heights), dims[position] // parts).reshape((-1,) + (1,) * (len(dims) - position - 1))

    level = one(*cuts[0])
    for cut in cuts[1:]:
        level = level * one(*cut)
    return level


def routed_block(key, own, number, rows, count, top, limit, lean):
    order = jax.random.permutation(key, count)
    packed, ordinary = portions_of(count, rows * top, limit, lean, True), portions_of(count, rows * top, limit, lean, False)
    places = jnp.arange(count)

    def named(tallies, offset_by):
        used = int((tallies > 0).sum())
        fixed = max(1, used // 4)
        shifted = fixed + (places - fixed + offset_by * (used - fixed)) % max(1, count - fixed)
        return jnp.zeros((count,), jnp.int32).at[order[jnp.where(places < fixed, places, shifted)]].set(jnp.asarray(tallies, jnp.int32))

    tallies = jnp.where(number % 4 == 0, named(packed, number // 4), named(ordinary, number - number // 4 - 1))
    mixed = jax.random.permutation(jax.random.fold_in(own, 3), count)
    source_of, sink = mixed[0:count // 2 * 2:2], mixed[1:count // 2 * 2:2]
    room = jnp.minimum(tallies[source_of] - 1, limit - tallies[sink]) // 2
    room = jnp.where((source_of == order[0]) | (sink == order[0]) | (tallies[sink] == 0), 0, jnp.maximum(room, 0))
    shifted = jax.random.randint(jax.random.fold_in(own, 4), (count // 2,), 0, 1 << 20) % (room + 1)
    tallies = tallies.at[source_of].add(-shifted).at[sink].add(shifted)
    items = jnp.searchsorted(jnp.cumsum(tallies), jnp.arange(rows * top), side="right").astype(jnp.int32)
    listing = items.reshape(top, rows).T
    listing = listing[jax.random.permutation(jax.random.fold_in(own, 1), rows)]
    offset_by = jax.random.randint(jax.random.fold_in(own, 2), (rows, 1), 0, top)
    return jnp.take_along_axis(listing, (jnp.arange(top)[None, :] + offset_by) % top, axis=1)


def portions_of(amount, total, reach, slope, full):
    portions = [(1 << 20) // math.isqrt(grade ** slope) + 1 for grade in range(1, amount + 1)]
    largest = reach if full else min(reach, max(-(-total // amount), total * portions[0] // sum(portions)))
    least = 1 if total - largest >= amount - 1 else 0
    holding, surplus = [largest] + [least] * (amount - 1), total - largest - least * (amount - 1)
    while surplus > 0:
        free = [i for i in range(1, amount) if holding[i] < largest] or [i for i in range(1, amount) if holding[i] < reach]
        mass, left = sum([portions[i] for i in free]), surplus
        for i in free:
            more = min(reach - holding[i], max(1, left * portions[i] // mass), surplus)
            holding[i] = holding[i] + more
            surplus = surplus - more
    return np.array(holding)


def bell_draw(rng, extent, scale, reach, shards=(), held_as=jnp.bfloat16):
    drawn = jax.random.normal(rng, extent, jnp.float32) * scale
    if len(shards) > 0:
        drawn = steps_of(rng, extent, shards, -0.22, 0.18) * drawn
    return jnp.clip(drawn, min=-reach, max=reach).astype(held_as)


def setup_inputs(seed: int = 0) -> dict:
    arg_keys = jax.random.split(jax.random.key(seed), 9)
    points = bell_draw(arg_keys[0], (POINTS, D), 1.0, 6.0, ((0, 512),))
    owner_block_keys = jax.random.split(jax.random.fold_in(arg_keys[1], 1), POINTS // P_DEV)
    owner_block_turns = jax.random.permutation(jax.random.fold_in(arg_keys[1], 3), POINTS // P_DEV)
    owner_block = jax.vmap(lambda own, number: routed_block(jax.random.fold_in(arg_keys[1], 2), own, number, P_DEV, BLOCKS, 1, CAP, 2))(owner_block_keys, owner_block_turns).reshape((POINTS, 1))
    centroid_slot = set_ends(jax.random.randint(arg_keys[2], (POINTS,), 0, K1_CENT), jax.random.fold_in(arg_keys[2], 1), 0, K1_CENT - 1).astype(jnp.int32)
    old_first = bell_draw(arg_keys[3], (K1, D), 1.0, 6.0, ((0, 512),))
    group_second = set_ends(jax.random.randint(arg_keys[4], (K1,), 0, K2), jax.random.fold_in(arg_keys[4], 1), 0, K2 - 1).astype(jnp.int32)
    group_third = set_ends(jax.random.randint(arg_keys[5], (K2,), 0, K3), jax.random.fold_in(arg_keys[5], 1), 0, K3 - 1).astype(jnp.int32)
    old_second = bell_draw(arg_keys[6], (K2, D), 1.0, 6.0)
    old_third = bell_draw(arg_keys[7], (K3, D), 1.0, 6.0)
    return dict(points=points, owner_block=owner_block, centroid_slot=centroid_slot, old_first=old_first, group_second=group_second, group_third=group_third, old_second=old_second, old_third=old_third)


def normalize(vector):
    return vector * lax.rsqrt(lax.optimization_barrier(jnp.mean(vector * vector, axis=-1, keepdims=True)) + 1e-06)

def update(summed, previous):
    return normalize(normalize(summed) + previous.astype(jnp.float32)).astype(jnp.bfloat16)

def reference(points, owner_block, centroid_slot, old_first, group_second, group_third, old_second, old_third):
    owners = owner_block[:, 0].astype(jnp.int32)
    centroid_ids = (centroid_slot // R1 * (BLOCKS * R1) + owners * R1 + centroid_slot % R1).astype(jnp.int32)
    block_size = math.gcd(POINTS, 8192)
    block_count = POINTS // block_size
    point_blocks = points.reshape(block_count, block_size, D)
    id_blocks = centroid_ids.reshape(block_count, block_size)

    def accumulate(summed, block_pair):
        block_points, block_ids = block_pair
        return (summed + jax.ops.segment_sum(block_points.astype(jnp.float32), block_ids, num_segments=K1), None)
    first_sum, _ = lax.scan(accumulate, jnp.zeros((K1, D), jnp.float32), (point_blocks, id_blocks))
    first_centroids = update(first_sum, old_first)
    second_sum = jax.ops.segment_sum(first_sum, group_second, num_segments=K2)
    second_centroids = update(second_sum, old_second)
    third_sum = jax.ops.segment_sum(second_sum, group_third, num_segments=K3)
    third_centroids = update(third_sum, old_third)
    centroid_table = first_centroids.astype(jnp.float32)
    score_scale = 1.0 / math.sqrt(D)

    def block_best(block_points):
        scores = jnp.dot(block_points.astype(jnp.float32), centroid_table.T, precision=lax.Precision.HIGHEST) * score_scale
        return lax.optimization_barrier(jnp.max(scores, axis=1))
    best_scores = lax.map(block_best, point_blocks).reshape(POINTS)
    return (first_centroids, second_centroids, third_centroids, best_scores)
```

```python
import functools
import math

import jax
import jax.numpy as jnp
from jax import lax
from jax.experimental import pallas as pl
from jax.experimental.pallas import tpu as pltpu
from jax.sharding import PartitionSpec as P

MESH = pl.DeviceIdType.MESH
F32, BF16, I32 = jnp.float32, jnp.bfloat16, jnp.int32

NX = 4
NR = 8
ZLO = 2
ZHI = NR // ZLO
R1 = 4
K2 = 256
K3 = 16
CAP = 32
ROWS = ZHI * CAP


def iota(shape, axis):
    return lax.broadcasted_iota(I32, shape, axis)


def dot(a, b, contract=((1,), (0,)), **kw):
    return lax.dot_general(a, b, (contract, ((), ())), preferred_element_type=F32, **kw)


def kernel(
    points, owners, slots, old_first, ids, third_ids, old_second, old_third,
    first_out, second_out, third_out, best_out,
    packed, packed_keys, rows, keys, sibling_points, id_tile, id_y, id_mid, id_z, id_half, id_sib,
    sums, land_a, mid, land_b, cent_tile, land_cx, second_tile, cents, seconds, sib_seconds,
    second_sum, best_tile, best_land, send_sem, recv_sem,
):
    dp, cent = lax.axis_index("dp"), lax.axis_index("cent")
    c = lax.rem(dp, 2)
    zlo = lax.rem(lax.div(dp, 2), ZLO)
    y = lax.div(dp, 2 * ZLO)
    x = lax.div(cent, ZHI)
    z = lax.rem(cent, ZHI) * ZLO + zlo
    a = y + c * (z - y)
    b = z + c * (y - z)
    slot_count = NR * ZLO * 2 * R1
    n_points, width = points.shape

    def device(x_, y_, z_, c_):
        return ((y_ * ZLO + lax.rem(z_, ZLO)) * 2 + c_, x_ * ZHI + lax.div(z_, ZLO))

    def on_x(o):
        return device(lax.rem(x + o, NX), y, z, c)

    def on_y(o):
        return device(x, lax.rem(y + o, NR), z, c)

    def on_z(o):
        return device(x, y, lax.rem(z + o, NR), c)

    def on_a(o):
        t = lax.rem(a + o, NR)
        return device(x, y + (1 - c) * (t - y), z + c * (t - z), c)

    def on_b(o):
        t = lax.rem(b + o, NR)
        return device(x, y + c * (t - y), z + (1 - c) * (t - z), c)

    sibling = device(x, y, z, 1 - c)

    barrier = pltpu.get_barrier_semaphore()
    partners = [sibling]
    partners += [on_x(o) for o in range(1, NX)]
    partners += [on_y(o) for o in range(1, NR)]
    partners += [on_z(o) for o in range(1, NR)]
    for partner in partners:
        pl.semaphore_signal(barrier, inc=1, device_id=partner, device_id_type=MESH)

    started = []

    def send(src, dst, target):
        n = len(started)
        copy = pltpu.make_async_remote_copy(
            src_ref=src, dst_ref=dst, send_sem=send_sem.at[n], recv_sem=recv_sem.at[n],
            device_id=target, device_id_type=MESH,
        )
        copy.start()
        started.append(copy)
        return copy

    base = ((y * ZLO + zlo) * 2 + c) * R1
    tile = jnp.zeros(id_tile.shape, I32)
    for r in range(R1):
        here = (iota(id_tile.shape, 0) == lax.div(z, ZLO)) & (iota(id_tile.shape, 1) == base + r)
        tile = tile + jnp.where(here, ids[r], 0)
    id_tile[...] = tile

    owner = owners[...]
    rel = lax.rem(lax.div(owner, ZHI) - x + NX, NX)
    key = lax.rem(owner, ZHI) * slot_count + slots[...]
    choose = (iota((16, n_points), 0) == rel).astype(F32)
    before = (iota((n_points, n_points), 0) < iota((n_points, n_points), 1)).astype(BF16)
    ranks = dot(choose.astype(BF16), before)
    rank = jnp.sum(ranks * choose, axis=0, keepdims=True).astype(I32)
    spot = rel * ROWS + rank
    place = (iota((NX * ROWS, n_points), 0) == spot).astype(F32).astype(BF16)
    which = iota((16, n_points), 0)
    parts = jnp.where(which == 0, lax.div(key, 16), jnp.where(which == 1, lax.rem(key, 16), 1))
    key_rows = dot(parts.astype(F32).astype(BF16), place, ((1,), (1,)))
    key_row = jnp.where(key_rows[2:3] > 0.5, key_rows[0:1] * 16.0 + key_rows[1:2], -1.0)
    for o in range(NX):
        block = dot(place[o * ROWS:(o + 1) * ROWS], points[...]).astype(BF16)
        block_keys = jnp.broadcast_to(key_row[:, o * ROWS:(o + 1) * ROWS], (8, ROWS))
        if o == 0:
            rows[0] = block
            keys[0] = block_keys
        else:
            packed[o - 1] = block
            packed_keys[o - 1] = block_keys

    pl.semaphore_wait(barrier, len(partners))

    over_x = []
    for o in range(1, NX):
        over_x.append((
            send(packed_keys.at[o - 1], keys.at[o], on_x(o)),
            send(packed.at[o - 1], rows.at[o], on_x(o)),
        ))
    over_y = [send(id_tile, id_y.at[o - 1], on_y(o)) for o in range(1, NR)]
    forward = [(
        send(keys.at[0], keys.at[NX], sibling),
        send(rows.at[0], rows.at[NX], sibling),
    )]
    whole_points = send(points, sibling_points, sibling)

    for copy in over_y:
        copy.wait_recv()
    id_mid[...] = id_tile[...] + jnp.sum(id_y[...], axis=0)
    over_z = [send(id_mid, id_z.at[o - 1], on_z(o)) for o in range(1, NR)]
    for copy in over_z:
        copy.wait_recv()
    id_half[...] = id_mid[...] + jnp.sum(id_z[...], axis=0)
    ids_copy = send(id_half, id_sib, sibling)
    ids_copy.wait_recv()
    id_all = (id_half[...] + id_sib[...]).astype(F32)
    id_row = jnp.concatenate([id_all[h:h + 1, :] for h in range(ZHI)], axis=1)
    id_row = jnp.broadcast_to(id_row, (16, ZHI * slot_count)).astype(BF16)

    for o in range(1, NX):
        for copy in over_x[o - 1]:
            copy.wait_recv()
        forward.append((
            send(keys.at[o], keys.at[NX + o], sibling),
            send(rows.at[o], rows.at[NX + o], sibling),
        ))

    count = NR * NR * 8
    half, quarter = width // 2, width // 4
    lanes = NX * ROWS
    row = iota((count, 1), 0)
    ta = lax.rem(a + lax.div(row, NR * 8), NR)
    tb = lax.rem(b + lax.rem(lax.div(row, 8), NR), NR)
    ty = ta + c * (tb - ta)
    tz = tb + c * (ta - tb)
    within = lax.rem(row, 8)
    slot = ((ty * ZLO + lax.rem(tz, ZLO)) * 2 + c) * R1 + lax.rem(within, R1)
    key_of = lax.div(tz, ZLO) * slot_count + slot
    group_of = lax.rem(within, 2) * (2 * NR * NR) + c * (NR * NR) + ta * NR + tb

    def one_hot(of, here, values):
        of = jnp.where(here, of, -2)
        return (of == values).astype(F32).astype(BF16)

    for core in range(2):
        if core == 1:
            for pair in forward:
                for copy in pair:
                    copy.wait_recv()
        span = range(core * NX, (core + 1) * NX)
        key_row = jnp.concatenate([keys[i, 0:1, :] for i in span], axis=1).astype(I32)
        full = (iota((ZHI * slot_count, lanes), 0) == key_row).astype(F32).astype(BF16)
        groups = dot(id_row, full)[0:1].astype(I32)
        held = rows[core * NX:(core + 1) * NX].reshape(lanes, width)
        first = dot(one_hot(key_of, within < R1, key_row), held[:, :half])
        first = first + dot(one_hot(key_of, within >= R1, key_row), held[:, half:])
        second = jnp.zeros((count, quarter), F32)
        for q in range(4):
            pick = one_hot(group_of, lax.div(within, 2) == q, groups)
            second = second + dot(pick, held[:, q * quarter:(q + 1) * quarter])
        first = first.reshape(NR, NR * 8, half)
        second = second.reshape(NR, NR * 8, quarter)
        if core == 0:
            sums[:, :, :half] = first
            sums[:, :, half:] = second
        else:
            sums[:, :, :half] = sums[:, :, :half] + first
            sums[:, :, half:] = sums[:, :, half:] + second

    over_a = [send(sums.at[o], land_a.at[o - 1], on_a(o)) for o in range(1, NR)]
    total = sums[0]
    for o in range(1, NR):
        over_a[o - 1].wait_recv()
        total = total + land_a[o - 1]
    mid[...] = total.reshape(mid.shape)
    over_b = [send(mid.at[o], land_b.at[o - 1], on_b(o)) for o in range(1, NR)]
    total = mid[0]
    for o in range(1, NR):
        over_b[o - 1].wait_recv()
        total = total + land_b[o - 1]

    def scale_of(v):
        squares = jnp.sum(v * v, axis=1, keepdims=True)
        squares = squares[:R1] + squares[R1:]
        return lax.rsqrt(jnp.concatenate([squares, squares], axis=0) / width + 1e-06)

    first = total[:, :half]
    old = old_first[...].astype(F32)
    old = jnp.concatenate([old[:, :half], old[:, half:]], axis=0)
    first = first * scale_of(first) + old
    first = first * scale_of(first)
    first = jnp.concatenate([first[:R1], first[R1:]], axis=1)
    first_out[...] = first.astype(BF16)
    spread = jnp.concatenate([first] * NX, axis=0)
    spread = jnp.where(lax.div(iota((NX * R1, 1), 0), R1) == x, spread, 0.0)
    cent_tile[...] = spread.astype(BF16)
    second_tile[x] = total[:, half:]
    gather_x = []
    for o in range(1, NX):
        gather_x.append(send(cent_tile, land_cx.at[o - 1], on_x(o)))
        gather_x.append(send(second_tile.at[x], second_tile.at[x], on_x(o)))
    for copy in gather_x:
        copy.wait_recv()
    for o in range(1, NX):
        spread = spread + land_cx[o - 1].astype(F32)
    cents[a, b] = spread.astype(BF16)
    second = second_tile[0]
    for o in range(1, NX):
        second = second + second_tile[o]
    lane = quarter // 2
    seconds[a, b] = jnp.concatenate([second[:, :lane], second[:, lane:]], axis=0)

    gather_b = []
    for o in range(1, NR):
        gather_b.append(send(cents.at[a, b], cents.at[a, b], on_b(o)))
        gather_b.append(send(seconds.at[a, b], seconds.at[a, b], on_b(o)))
    for copy in gather_b:
        copy.wait_recv()

    whole_points.wait_recv()
    best = [None, None]

    def score(blocks):
        block = blocks.reshape(-1, width)
        for i, held in enumerate((points, sibling_points)):
            s = dot(block, held[...], ((1,), (1,)))
            s = jnp.max(s.reshape(-1, 8, n_points), axis=0)
            best[i] = s if best[i] is None else jnp.maximum(best[i], s)

    right, left = on_a(1), on_a(NR - 1)
    hop = NR // 2
    waiting = []
    for step in range(1, hop + 1):
        from_left = lax.rem(a - step + 1 + NR, NR)
        from_right = lax.rem(a + step - 1, NR)
        for copy in waiting:
            copy.wait_recv()
        waiting = []
        for buffer in (cents, seconds):
            if step < hop:
                waiting.append(send(buffer.at[from_left], buffer.at[from_left], right))
                waiting.append(send(buffer.at[from_right], buffer.at[from_right], left))
            else:
                part = buffer.at[from_left, pl.ds(0, NR // 2)]
                waiting.append(send(part, part, right))
                part = buffer.at[from_right, pl.ds(NR // 2, NR // 2)]
                waiting.append(send(part, part, left))
        if step == 1:
            score(cents[a])
        else:
            score(cents[from_left])
            score(cents[from_right])
    for copy in waiting:
        copy.wait_recv()
    seconds_copy = send(seconds, sib_seconds, sibling)
    score(cents[lax.rem(a + hop, NR)])
    best_tile[...] = best[1]
    best_copy = send(best_tile, best_land, sibling)

    seconds_copy.wait_recv()
    per = NR * NR
    for r in range(2):
        for i in range(8):
            picked = pl.ds((i % 2) * 8 + (i // 2) * 2 + r, per, stride=16)
            own = seconds.reshape(per * 16, lane)[picked, :]
            other = sib_seconds.reshape(per * 16, lane)[picked, :]
            cols = slice(i * lane, (i + 1) * lane)
            second_sum[(2 * r) * per:(2 * r + 1) * per, cols] = jnp.where(c == 0, own, other)
            second_sum[(2 * r + 1) * per:(2 * r + 2) * per, cols] = jnp.where(c == 0, other, own)

    def normalize(v):
        return v * lax.rsqrt(jnp.mean(v * v, axis=1, keepdims=True) + 1e-06)

    second = second_sum[...]
    second_out[...] = normalize(normalize(second) + old_second[...].astype(F32)).astype(BF16)
    pick = (iota((K3, K2), 0) == third_ids[...]).astype(F32)
    third = dot(pick, second, precision=lax.Precision.HIGHEST)
    third_out[...] = normalize(normalize(third) + old_third[...].astype(F32)).astype(BF16)

    best_copy.wait_recv()
    top = jnp.max(jnp.maximum(best[0], best_land[...]), axis=0, keepdims=True)
    best_out[...] = top * (1.0 / math.sqrt(width))
    for copy in started:
        copy.wait_send()


def body(
    points, owner_block, centroid_slot, old_first, group_second, group_third, old_second, old_third
):
    n_points, width = points.shape
    half, quarter = width // 2, width // 4
    slot_count = NR * ZLO * 2 * R1
    vmem = pl.BlockSpec(memory_space=pltpu.VMEM)
    smem = pl.BlockSpec(memory_space=pltpu.SMEM)
    copies = 160
    first, second, third, best = pl.pallas_call(
        kernel,
        out_shape=(
            jax.ShapeDtypeStruct((R1, width), BF16),
            jax.ShapeDtypeStruct((K2, width), BF16),
            jax.ShapeDtypeStruct((K3, width), BF16),
            jax.ShapeDtypeStruct((1, n_points), F32),
        ),
        in_specs=[vmem, vmem, vmem, vmem, smem, vmem, vmem, vmem],
        out_specs=(vmem, vmem, vmem, vmem),
        scratch_shapes=[
            pltpu.VMEM((NX - 1, ROWS, width), BF16),
            pltpu.VMEM((NX - 1, 8, ROWS), F32),
            pltpu.VMEM((2 * NX, ROWS, width), BF16),
            pltpu.VMEM((2 * NX, 8, ROWS), F32),
            pltpu.VMEM((n_points, width), BF16),
            pltpu.VMEM((8, slot_count), I32),
            pltpu.VMEM((NR - 1, 8, slot_count), I32),
            pltpu.VMEM((8, slot_count), I32),
            pltpu.VMEM((NR - 1, 8, slot_count), I32),
            pltpu.VMEM((8, slot_count), I32),
            pltpu.VMEM((8, slot_count), I32),
            pltpu.VMEM((NR, NR * 8, half + quarter), F32),
            pltpu.VMEM((NR - 1, NR * 8, half + quarter), F32),
            pltpu.VMEM((NR, 8, half + quarter), F32),
            pltpu.VMEM((NR - 1, 8, half + quarter), F32),
            pltpu.VMEM((NX * R1, width), BF16),
            pltpu.VMEM((NX - 1, NX * R1, width), BF16),
            pltpu.VMEM((NX, 8, quarter), F32),
            pltpu.VMEM((NR, NR, NX * R1, width), BF16),
            pltpu.VMEM((NR, NR, 16, quarter // 2), F32),
            pltpu.VMEM((NR, NR, 16, quarter // 2), F32),
            pltpu.VMEM((K2, width), F32),
            pltpu.VMEM((8, n_points), F32),
            pltpu.VMEM((8, n_points), F32),
            pltpu.SemaphoreType.DMA((copies,)),
            pltpu.SemaphoreType.DMA((copies,)),
        ],
        compiler_params=pltpu.CompilerParams(
            collective_id=0, has_side_effects=True, vmem_limit_bytes=48 * 1024 * 1024
        ),
    )(
        points,
        owner_block.reshape(1, n_points),
        centroid_slot.reshape(1, n_points),
        old_first,
        group_second,
        group_third.reshape(1, K2),
        old_second,
        old_third,
    )
    return first, second, third, best.reshape(n_points)


def solution(mesh):
    in_specs = (
        P(("dp", "cent"), None),
        P(("dp", "cent"), None),
        P(("dp", "cent")),
        P(("dp", "cent"), None),
        P(("dp", "cent")),
        P(),
        P(),
        P(),
    )
    out_specs = (P(("dp", "cent"), None), P(), P(), P(("dp", "cent")))
    return jax.shard_map(body, mesh=mesh, in_specs=in_specs, out_specs=out_specs, check_vma=False)
```

```python
import math

import jax
import jax.numpy as jnp
from jax import lax
from jax.experimental import pallas as pl
from jax.experimental.pallas import tpu as pltpu
from jax.sharding import PartitionSpec as P

MESH = pl.DeviceIdType.MESH
F32, BF16, I32 = jnp.float32, jnp.bfloat16, jnp.int32

NX = 4
NR = 8
ZLO = 2
ZHI = NR // ZLO
R1 = 4
K2 = 256
K3 = 16
CAP = 32
ROWS = ZHI * CAP


def iota(shape, axis):
    return lax.broadcasted_iota(I32, shape, axis)


def dot(a, b, contract=((1,), (0,)), **kw):
    return lax.dot_general(a, b, (contract, ((), ())), preferred_element_type=F32, **kw)


FAR = (4, 3, 5, 2, 6, 1, 7)


def kernel(
    points_in, owners, slots, old_first_in, ids, third_ids, old_second_in, old_third_in,
    first_out, second_out, third_out, best_out,
    points, old_first, old_second, old_third, packed, packed_keys, rows, keys,
    raw, sib_raw, turned, id_tile, id_y, id_mid, id_z, id_half, id_sib,
    sums, land_a, mid, land_b, halves, land_halves, spread, land_spread, mid_second, land_second,
    second_tile, cents_b, cents, seconds, sib_seconds, second_sum, best_tile, best_land,
    local_sem, send_sem, recv_sem,
):
    fetches = [
        pltpu.make_async_copy(src, dst, local_sem.at[n])
        for n, (src, dst) in enumerate((
            (points_in, points), (old_first_in, old_first),
            (old_second_in, old_second), (old_third_in, old_third),
        ))
    ]
    for fetch in fetches:
        fetch.start()

    dp, cent = lax.axis_index("dp"), lax.axis_index("cent")
    c = lax.rem(dp, 2)
    zlo = lax.rem(lax.div(dp, 2), ZLO)
    y = lax.div(dp, 2 * ZLO)
    x = lax.div(cent, ZHI)
    z = lax.rem(cent, ZHI) * ZLO + zlo
    a = y + c * (z - y)
    b = z + c * (y - z)
    slot_count = NR * ZLO * 2 * R1
    n_points, width = points.shape
    half, quarter = width // 2, width // 4
    lane = 128

    def device(x_, y_, z_, c_):
        return ((y_ * ZLO + lax.rem(z_, ZLO)) * 2 + c_, x_ * ZHI + lax.div(z_, ZLO))

    def on_x(o, core=0):
        return device(lax.rem(x + o + NX, NX), y, z, lax.rem(c + core, 2))

    def on_y(o):
        return device(x, lax.rem(y + o, NR), z, c)

    def on_z(o):
        return device(x, y, lax.rem(z + o, NR), c)

    def on_a(o):
        t = lax.rem(a + o, NR)
        return device(x, y + (1 - c) * (t - y), z + c * (t - z), c)

    def on_b(o):
        t = lax.rem(b + o, NR)
        return device(x, y + c * (t - y), z + (1 - c) * (t - z), c)

    sibling = device(x, y, z, 1 - c)

    barrier = pltpu.get_barrier_semaphore()
    partners = [sibling]
    partners += [on_x(o, core) for o in range(1, NX) for core in range(2)]
    partners += [on_y(o) for o in range(1, NR)]
    partners += [on_z(o) for o in range(1, NR)]
    for partner in partners:
        pl.semaphore_signal(barrier, inc=1, device_id=partner, device_id_type=MESH)

    started = []

    def send(src, dst, target):
        n = len(started)
        copy = pltpu.make_async_remote_copy(
            src_ref=src, dst_ref=dst, send_sem=send_sem.at[n], recv_sem=recv_sem.at[n],
            device_id=target, device_id_type=MESH,
        )
        copy.start()
        started.append(copy)
        return copy

    def arrive(copies):
        for copy in copies:
            copy.wait_recv()

    base = ((y * ZLO + zlo) * 2 + c) * R1
    tile = jnp.zeros(id_tile.shape, I32)
    for r in range(R1):
        here = (iota(id_tile.shape, 0) == lax.div(z, ZLO)) & (iota(id_tile.shape, 1) == base + r)
        tile = tile + jnp.where(here, ids[r], 0)
    id_tile[...] = tile

    owner = owners[...]
    rel = lax.rem(lax.div(owner, ZHI) - x + NX, NX)
    key = lax.rem(owner, ZHI) * slot_count + slots[...]
    choose = (iota((16, n_points), 0) == rel).astype(F32)
    before = (iota((n_points, n_points), 0) < iota((n_points, n_points), 1)).astype(BF16)
    ranks = dot(choose.astype(BF16), before)
    rank = jnp.sum(ranks * choose, axis=0, keepdims=True).astype(I32)
    spot = rel * ROWS + rank
    place = (iota((NX * ROWS, n_points), 0) == spot).astype(F32).astype(BF16)
    which = iota((16, n_points), 0)
    parts = jnp.where(which == 0, lax.div(key, 16), jnp.where(which == 1, lax.rem(key, 16), 1))
    key_rows = dot(parts.astype(F32).astype(BF16), place, ((1,), (1,)))
    key_row = jnp.where(key_rows[2:3] > 0.5, key_rows[0:1] * 16.0 + key_rows[1:2], -1.0)
    fetches[0].wait()
    for o in range(NX):
        block = dot(place[o * ROWS:(o + 1) * ROWS], points[...]).astype(BF16)
        block_keys = jnp.broadcast_to(key_row[:, o * ROWS:(o + 1) * ROWS], (8, ROWS))
        if o == 0:
            rows[0] = block
            keys[0] = block_keys
        else:
            packed[o - 1] = block
            packed_keys[o - 1] = block_keys

    pl.semaphore_wait(barrier, len(partners))

    over_x = {}
    for o in (2, 1, 3):
        over_x[o] = (
            send(packed_keys.at[o - 1], keys.at[o], on_x(o)),
            send(packed.at[o - 1], rows.at[o], on_x(o)),
        )
    over_y = [send(id_tile, id_y.at[o - 1], on_y(o)) for o in range(1, NR)]
    forward = [(
        send(keys.at[0], keys.at[NX], sibling),
        send(rows.at[0], rows.at[NX], sibling),
    )]
    raw_own = send(points, sib_raw.at[0], sibling)

    spread[...] = jnp.zeros(spread.shape, F32)
    turned[0] = points[...].T
    arrive(over_y)
    id_mid[...] = id_tile[...] + jnp.sum(id_y[...], axis=0)
    over_z = [send(id_mid, id_z.at[o - 1], on_z(o)) for o in range(1, NR)]
    arrive(over_z)
    id_half[...] = id_mid[...] + jnp.sum(id_z[...], axis=0)
    ids_copy = send(id_half, id_sib, sibling)
    ids_copy.wait_recv()
    id_all = (id_half[...] + id_sib[...]).astype(F32)
    id_row = jnp.concatenate([id_all[h:h + 1, :] for h in range(ZHI)], axis=1)
    id_row = jnp.broadcast_to(id_row, (16, ZHI * slot_count)).astype(BF16)
    raw_own.wait_recv()
    turned[NX] = sib_raw[0].T

    for o in (1, 3, 2):
        arrive(over_x[o])
        forward.append((
            send(keys.at[o], keys.at[NX + o], sibling),
            send(rows.at[o], rows.at[NX + o], sibling),
        ))
    raw_x = {o: send(points, raw.at[o - 1], on_x(o)) for o in (1, 3)}

    count = NR * NR * 8
    lanes = NX * ROWS
    row = iota((count, 1), 0)
    ta = lax.rem(a + lax.div(row, NR * 8), NR)
    tb = lax.rem(b + lax.rem(lax.div(row, 8), NR), NR)
    ty = ta + c * (tb - ta)
    tz = tb + c * (ta - tb)
    within = lax.rem(row, 8)
    slot = ((ty * ZLO + lax.rem(tz, ZLO)) * 2 + c) * R1 + lax.rem(within, R1)
    key_of = lax.div(tz, ZLO) * slot_count + slot
    left_key = jnp.where(within < R1, key_of, -2)
    right_key = jnp.where(within >= R1, key_of, -2)

    def one_hot(of, values):
        return (of == values).astype(F32).astype(BF16)

    all_keys = []
    for core in range(2):
        if core == 1:
            for pair in forward:
                arrive(pair)
        span = range(core * NX, (core + 1) * NX)
        key_row = jnp.concatenate([keys[i, 0:1, :] for i in span], axis=1).astype(I32)
        all_keys.append(key_row)
        held = rows[core * NX:(core + 1) * NX].reshape(lanes, width)
        first = dot(one_hot(left_key, key_row), held[:, :half])
        first = first + dot(one_hot(right_key, key_row), held[:, half:])
        first = first.reshape(NR, NR * 8, half)
        if core == 0:
            sums[...] = first
        else:
            sums[...] = sums[...] + first
    over_a = {o: send(sums.at[o], land_a.at[o - 1], on_a(o)) for o in FAR}

    pairs = NR * NR
    row = iota((2 * pairs, 1), 0)
    ta = lax.rem(a + lax.rem(row, NR), NR)
    tb = lax.rem(b + lax.rem(lax.div(row, NR), NR), NR)
    group_of = lax.div(row, pairs) * (2 * pairs) + c * pairs + tb * NR + ta
    second = jnp.zeros((2 * pairs, width), F32)
    for core in range(2):
        full = one_hot(iota((ZHI * slot_count, lanes), 0), all_keys[core])
        groups = dot(id_row, full)[0:1].astype(I32)
        held = rows[core * NX:(core + 1) * NX].reshape(lanes, width)
        second = second + dot(one_hot(group_of, groups), held)
    for q in range(NX):
        halves[lax.rem(q - x + NX, NX)] = second[:, q * quarter:(q + 1) * quarter]
    second_x = [send(halves.at[o], land_halves.at[o - 1], on_x(o)) for o in (2, 1, 3)]
    arrive(second_x)
    raw_x[2] = send(points, raw.at[1], on_x(2))
    second = halves[0]
    for o in range(1, NX):
        second = second + land_halves[o - 1]
    flat = spread.reshape(pairs * 8, lane)
    for h in range(2):
        for r in range(2):
            flat[pl.ds(h * 2 + r, pairs, stride=8), :] = second[
                r * pairs:(r + 1) * pairs, h * lane:(h + 1) * lane
            ]
    second_b = [send(spread.at[o], land_spread.at[o - 1], on_b(o)) for o in FAR]

    total = sums[0]
    for o in range(1, NR):
        over_a[o].wait_recv()
        total = total + land_a[o - 1]
    mid[...] = total.reshape(mid.shape)
    over_b = {o: send(mid.at[o], land_b.at[o - 1], on_b(o)) for o in FAR}
    forward_raw = []
    for o in (1, 3):
        raw_x[o].wait_recv()
        forward_raw.append(send(raw.at[o - 1], sib_raw.at[o], sibling))
        turned[o] = raw[o - 1].T
    arrive(second_b)
    second = spread[0]
    for o in range(1, NR):
        second = second + land_spread[o - 1]
    mid_second[...] = second.reshape(mid_second.shape)
    second_a = [send(mid_second.at[o], land_second.at[o - 1], on_a(o)) for o in FAR]
    total = mid[0]
    for o in range(1, NR):
        over_b[o].wait_recv()
        total = total + land_b[o - 1]

    def scale_of(v):
        squares = jnp.sum(v * v, axis=1, keepdims=True)
        squares = squares[:R1] + squares[R1:]
        return lax.rsqrt(jnp.concatenate([squares, squares], axis=0) / width + 1e-06)

    fetches[1].wait()
    old = old_first[...].astype(F32)
    old = jnp.concatenate([old[:, :half], old[:, half:]], axis=0)
    first = total * scale_of(total) + old
    first = first * scale_of(first)
    first = jnp.concatenate([first[:R1], first[R1:]], axis=1)
    first_out[...] = first.astype(BF16)
    cents_b[b] = jnp.concatenate(
        [first[:, q * quarter:(q + 1) * quarter] for q in range(4)], axis=0
    ).astype(BF16)
    gather_b = [send(cents_b.at[b], cents_b.at[b], on_b(o)) for o in FAR]

    arrive(second_a)
    second = mid_second[0]
    for o in range(1, NR):
        second = second + land_second[o - 1]
    second_tile[x] = second
    second_all = [send(second_tile.at[x], second_tile.at[x], on_x(o)) for o in (2, 1, 3)]
    arrive(second_all)
    seconds[b, a] = jnp.concatenate([second_tile[i, 0:4, :] for i in range(NX)], axis=0)
    seconds_a = [send(seconds.at[b, a], seconds.at[b, a], on_a(o)) for o in FAR]

    arrive(gather_b)
    per = NR * R1
    row = iota((4 * per, 1), 0)
    source = lax.div(lax.rem(row, per), R1) * 16 + lax.div(row, per) * R1 + lax.rem(row, R1)
    order = one_hot(source, iota((1, 4 * per), 1))
    block = dot(order, cents_b[...].reshape(4 * per, quarter)).astype(BF16)
    for q in range(4):
        cents[a, :, q * quarter:(q + 1) * quarter] = block[q * per:(q + 1) * per]
    gather_a = [send(cents.at[a], cents.at[a], on_a(o)) for o in FAR]
    arrive(seconds_a)
    seconds_b = [send(seconds.at[b], seconds.at[b], on_b(o)) for o in FAR]
    forward_second = [send(seconds.at[b], sib_seconds.at[b], sibling)]

    raw_x[2].wait_recv()
    forward_raw.append(send(raw.at[1], sib_raw.at[2], sibling))
    turned[2] = raw[1].T
    arrive(forward_raw)
    for o in range(1, NX):
        turned[NX + o] = sib_raw[o].T
    arrive(gather_a)

    table = cents[...].reshape(NR * per, width)
    best_copies = []
    own = None
    for g in (2, 6, 1, 3, 5, 7, 4, 0):
        s = jnp.max(dot(table, turned[g]).reshape(-1, 8, n_points), axis=0)
        if g == 0:
            own = s
        else:
            best_tile[g - 1] = s
            target = on_x(-(g % NX), g // NX)
            best_copies.append(send(best_tile.at[g - 1], best_land.at[g - 1], target))

    arrive(seconds_b)
    for o in range(1, NR):
        at = lax.rem(b + o, NR)
        forward_second.append(send(seconds.at[at], sib_seconds.at[at], sibling))
    fetches[2].wait()
    fetches[3].wait()
    arrive(forward_second)
    for r in range(2):
        for i in range(8):
            picked = pl.ds(i * 2 + r, pairs, stride=16)
            mine = seconds.reshape(pairs * 16, lane)[picked, :]
            other = sib_seconds.reshape(pairs * 16, lane)[picked, :]
            cols = slice(i * lane, (i + 1) * lane)
            second_sum[(2 * r) * pairs:(2 * r + 1) * pairs, cols] = jnp.where(c == 0, mine, other)
            second_sum[(2 * r + 1) * pairs:(2 * r + 2) * pairs, cols] = jnp.where(
                c == 0, other, mine
            )

    def normalize(v):
        return v * lax.rsqrt(jnp.mean(v * v, axis=1, keepdims=True) + 1e-06)

    second = second_sum[...]
    second_out[...] = normalize(normalize(second) + old_second[...].astype(F32)).astype(BF16)
    pick = (iota((K3, K2), 0) == third_ids[...]).astype(F32)
    third = dot(pick, second, precision=lax.Precision.HIGHEST)
    third_out[...] = normalize(normalize(third) + old_third[...].astype(F32)).astype(BF16)

    arrive(best_copies)
    top = jnp.maximum(own, jnp.max(best_land[...], axis=0))
    best_out[...] = jnp.max(top, axis=0, keepdims=True) * (1.0 / math.sqrt(width))
    for copy in started:
        copy.wait_send()


def body(
    points, owner_block, centroid_slot, old_first, group_second, group_third, old_second, old_third
):
    n_points, width = points.shape
    half, quarter = width // 2, width // 4
    slot_count = NR * ZLO * 2 * R1
    vmem = pl.BlockSpec(memory_space=pltpu.VMEM)
    smem = pl.BlockSpec(memory_space=pltpu.SMEM)
    hbm = pl.BlockSpec(memory_space=pltpu.HBM)
    copies = 160
    first, second, third, best = pl.pallas_call(
        kernel,
        out_shape=(
            jax.ShapeDtypeStruct((R1, width), BF16),
            jax.ShapeDtypeStruct((K2, width), BF16),
            jax.ShapeDtypeStruct((K3, width), BF16),
            jax.ShapeDtypeStruct((1, n_points), F32),
        ),
        in_specs=[hbm, vmem, vmem, hbm, smem, vmem, hbm, hbm],
        out_specs=(vmem, vmem, vmem, vmem),
        scratch_shapes=[
            pltpu.VMEM((n_points, width), BF16),
            pltpu.VMEM((R1, width), BF16),
            pltpu.VMEM((K2, width), BF16),
            pltpu.VMEM((K3, width), BF16),
            pltpu.VMEM((NX - 1, ROWS, width), BF16),
            pltpu.VMEM((NX - 1, 8, ROWS), F32),
            pltpu.VMEM((2 * NX, ROWS, width), BF16),
            pltpu.VMEM((2 * NX, 8, ROWS), F32),
            pltpu.VMEM((NX - 1, n_points, width), BF16),
            pltpu.VMEM((NX, n_points, width), BF16),
            pltpu.VMEM((2 * NX, width, n_points), BF16),
            pltpu.VMEM((8, slot_count), I32),
            pltpu.VMEM((NR - 1, 8, slot_count), I32),
            pltpu.VMEM((8, slot_count), I32),
            pltpu.VMEM((NR - 1, 8, slot_count), I32),
            pltpu.VMEM((8, slot_count), I32),
            pltpu.VMEM((8, slot_count), I32),
            pltpu.VMEM((NR, NR * 8, half), F32),
            pltpu.VMEM((NR - 1, NR * 8, half), F32),
            pltpu.VMEM((NR, 8, half), F32),
            pltpu.VMEM((NR - 1, 8, half), F32),
            pltpu.VMEM((NX, 2 * NR * NR, quarter), F32),
            pltpu.VMEM((NX - 1, 2 * NR * NR, quarter), F32),
            pltpu.VMEM((NR, NR * 8, 128), F32),
            pltpu.VMEM((NR - 1, NR * 8, 128), F32),
            pltpu.VMEM((NR, 8, 128), F32),
            pltpu.VMEM((NR - 1, 8, 128), F32),
            pltpu.VMEM((NX, 8, 128), F32),
            pltpu.VMEM((NR, 4 * R1, quarter), BF16),
            pltpu.VMEM((NR, NR * R1, width), BF16),
            pltpu.VMEM((NR, NR, 16, 128), F32),
            pltpu.VMEM((NR, NR, 16, 128), F32),
            pltpu.VMEM((K2, width), F32),
            pltpu.VMEM((2 * NX - 1, 8, n_points), F32),
            pltpu.VMEM((2 * NX - 1, 8, n_points), F32),
            pltpu.SemaphoreType.DMA((4,)),
            pltpu.SemaphoreType.DMA((copies,)),
            pltpu.SemaphoreType.DMA((copies,)),
        ],
        compiler_params=pltpu.CompilerParams(
            collective_id=0, has_side_effects=True, vmem_limit_bytes=56 * 1024 * 1024
        ),
    )(
        points,
        owner_block.reshape(1, n_points),
        centroid_slot.reshape(1, n_points),
        old_first,
        group_second,
        group_third.reshape(1, K2),
        old_second,
        old_third,
    )
    return first, second, third, best.reshape(n_points)


def solution(mesh):
    in_specs = (
        P(("dp", "cent"), None),
        P(("dp", "cent"), None),
        P(("dp", "cent")),
        P(("dp", "cent"), None),
        P(("dp", "cent")),
        P(),
        P(),
        P(),
    )
    out_specs = (P(("dp", "cent"), None), P(), P(), P(("dp", "cent")))
    return jax.shard_map(body, mesh=mesh, in_specs=in_specs, out_specs=out_specs, check_vma=False)
```

```python
import math

import jax
import jax.numpy as jnp
from jax import lax
from jax.experimental import pallas as pl
from jax.experimental.pallas import tpu as pltpu
from jax.sharding import PartitionSpec as P

MESH = pl.DeviceIdType.MESH
F32, BF16, I32 = jnp.float32, jnp.bfloat16, jnp.int32

NX = 4
NR = 8
ZLO = 2
ZHI = NR // ZLO
R1 = 4
K2 = 256
K3 = 16
CAP = 32
PARTS = 4
ROWS = ZHI * CAP


def iota(shape, axis):
    return lax.broadcasted_iota(I32, shape, axis)


def dot(a, b, contract=((1,), (0,)), **kw):
    return lax.dot_general(a, b, (contract, ((), ())), preferred_element_type=F32, **kw)


FAR = (4, 3, 5, 2, 6, 1, 7)


def kernel(
    points_in, owners, slots, old_first_in, ids, third_ids, old_second_in, old_third_in,
    first_out, second_out, third_out, best_out,
    points, old_first, old_second, old_third, packed, packed_keys, rows, keys, hot,
    raw, sib_raw, meta, sib_meta, turned, id_tile, id_y, id_mid, id_z, id_half, id_sib, id_full,
    sums, land_a, mid, land_b, halves, land_halves, spread, land_spread, over_second,
    cents_b, cents, compact, sib_compact, second_sum, best_tile, best_land,
    local_sem, send_sem, recv_sem,
):
    fetches = [
        pltpu.make_async_copy(src, dst, local_sem.at[n])
        for n, (src, dst) in enumerate((
            (points_in, points), (old_first_in, old_first),
            (old_second_in, old_second), (old_third_in, old_third),
        ))
    ]
    for fetch in fetches:
        fetch.start()

    dp, cent = lax.axis_index("dp"), lax.axis_index("cent")
    c = lax.rem(dp, 2)
    zlo = lax.rem(lax.div(dp, 2), ZLO)
    y = lax.div(dp, 2 * ZLO)
    x = lax.div(cent, ZHI)
    z = lax.rem(cent, ZHI) * ZLO + zlo
    a = y + c * (z - y)
    b = z + c * (y - z)
    slot_count = NR * ZLO * 2 * R1
    n_points, width = points.shape
    quarter = width // 4
    step = width // PARTS
    wide = step // 2
    groups_here = K2 // 2 // NR

    def device(x_, y_, z_, c_):
        return ((y_ * ZLO + lax.rem(z_, ZLO)) * 2 + c_, x_ * ZHI + lax.div(z_, ZLO))

    def on_x(o, core=0):
        return device(lax.rem(x + o + NX, NX), y, z, lax.rem(c + core, 2))

    def on_y(o):
        return device(x, lax.rem(y + o, NR), z, c)

    def on_z(o):
        return device(x, y, lax.rem(z + o, NR), c)

    def on_a(o):
        t = lax.rem(a + o, NR)
        return device(x, y + (1 - c) * (t - y), z + c * (t - z), c)

    def on_b(o):
        t = lax.rem(b + o, NR)
        return device(x, y + c * (t - y), z + (1 - c) * (t - z), c)

    sibling = device(x, y, z, 1 - c)

    barrier = pltpu.get_barrier_semaphore()
    partners = [sibling]
    partners += [on_x(o, core) for o in range(1, NX) for core in range(2)]
    partners += [on_y(o) for o in range(1, NR)]
    partners += [on_z(o) for o in range(1, NR)]
    for partner in partners:
        pl.semaphore_signal(barrier, inc=1, device_id=partner, device_id_type=MESH)

    started = []

    def send(src, dst, target):
        n = len(started)
        copy = pltpu.make_async_remote_copy(
            src_ref=src, dst_ref=dst, send_sem=send_sem.at[n], recv_sem=recv_sem.at[n],
            device_id=target, device_id_type=MESH,
        )
        copy.start()
        started.append(copy)
        return copy

    def arrive(copies):
        for copy in copies:
            copy.wait_recv()

    base = ((y * ZLO + zlo) * 2 + c) * R1
    tile = jnp.zeros(id_tile.shape, I32)
    for r in range(R1):
        here = (iota(id_tile.shape, 0) == lax.div(z, ZLO)) & (iota(id_tile.shape, 1) == base + r)
        tile = tile + jnp.where(here, ids[r], 0)
    id_tile[...] = tile

    owner = owners[...]
    rel = lax.rem(lax.div(owner, ZHI) - x + NX, NX)
    key = lax.rem(owner, ZHI) * slot_count + slots[...]
    choose = (iota((16, n_points), 0) == rel).astype(F32)
    before = (iota((n_points, n_points), 0) < iota((n_points, n_points), 1)).astype(BF16)
    ranks = dot(choose.astype(BF16), before)
    rank = jnp.sum(ranks * choose, axis=0, keepdims=True).astype(I32)
    spot = rel * ROWS + rank
    place = (iota((NX * ROWS, n_points), 0) == spot).astype(F32).astype(BF16)
    which = iota((16, n_points), 0)
    parts = jnp.where(which == 0, lax.div(key, 16), jnp.where(which == 1, lax.rem(key, 16), 1))
    key_rows = dot(parts.astype(F32).astype(BF16), place, ((1,), (1,)))
    key_row = jnp.where(key_rows[2:3] > 0.5, key_rows[0:1] * 16.0 + key_rows[1:2], -1.0)
    for o in range(NX):
        block_keys = jnp.broadcast_to(key_row[:, o * ROWS:(o + 1) * ROWS], (8, ROWS))
        if o == 0:
            keys[0] = block_keys
        else:
            packed_keys[o - 1] = block_keys
    meta[...] = jnp.where(iota(meta.shape, 0) == 0, owner, slots[...]).astype(F32)

    pl.semaphore_wait(barrier, len(partners))

    over_y = [send(id_tile, id_y.at[o - 1], on_y(o)) for o in range(1, NR)]
    keys_x = [send(packed_keys.at[o - 1], keys.at[o], on_x(o)) for o in (2, 1, 3)]
    forward_keys = [send(keys.at[0], keys.at[NX], sibling)]
    fetches[0].wait()
    over_x, forward = {}, {}
    for k in range(PARTS):
        cols = slice(k * step, (k + 1) * step)
        over_x[k] = []
        for o in (2, 1, 3, 0):
            block = dot(place[o * ROWS:(o + 1) * ROWS], points[:, cols]).astype(BF16)
            if o == 0:
                rows[k, 0] = block
                forward[k] = [send(rows.at[k, 0], rows.at[k, NX], sibling)]
            else:
                packed[k, o - 1] = block
                over_x[k].append(send(packed.at[k, o - 1], rows.at[k, o], on_x(o)))
    meta_copy = send(meta, sib_meta, sibling)
    raw_own = send(points, sib_raw.at[0], sibling)
    turned[0] = points[...].T

    arrive(over_y)
    id_mid[...] = id_tile[...] + jnp.sum(id_y[...], axis=0)
    over_z = [send(id_mid, id_z.at[o - 1], on_z(o)) for o in range(1, NR)]

    def one_hot(of, values):
        return (of == values).astype(F32).astype(BF16)

    count = NR * NR * 8
    lanes = NX * ROWS
    row = iota((count, 1), 0)
    ta = lax.rem(a + lax.div(row, NR * 8), NR)
    tb = lax.rem(b + lax.rem(lax.div(row, 8), NR), NR)
    ty = ta + c * (tb - ta)
    tz = tb + c * (ta - tb)
    within = lax.rem(row, 8)
    slot = ((ty * ZLO + lax.rem(tz, ZLO)) * 2 + c) * R1 + lax.rem(within, R1)
    key_of = lax.div(tz, ZLO) * slot_count + slot
    side_keys = (jnp.where(within < R1, key_of, -2), jnp.where(within >= R1, key_of, -2))

    def fill_hot(core):
        span = range(core * NX, (core + 1) * NX)
        key_row = jnp.concatenate([keys[i, 0:1, :] for i in span], axis=1).astype(I32)
        for side in range(2):
            hot[core, side] = one_hot(side_keys[side], key_row)

    def sum_part(k, core):
        held = rows[k, core * NX:(core + 1) * NX].reshape(lanes, step)
        part = dot(hot[core, 0], held[:, :wide]) + dot(hot[core, 1], held[:, wide:])
        return part.reshape(NR, NR * 8, wide)

    over_a = {}

    def finish_part(k):
        arrive(over_x[k])
        span = pl.ds(1, NX - 1)
        onward = pl.ds(NX + 1, NX - 1)
        forward[k].append(send(rows.at[k, span], rows.at[k, onward], sibling))
        sums[k] = sum_part(k, 0)
        arrive(forward[k])
        sums[k] = sums[k] + sum_part(k, 1)
        over_a[k] = {o: send(sums.at[k, o], land_a.at[k, o - 1], on_a(o)) for o in FAR}

    arrive(keys_x)
    for o in range(1, NX):
        forward_keys.append(send(keys.at[o], keys.at[NX + o], sibling))
    fill_hot(0)
    arrive(forward_keys)
    fill_hot(1)
    finish_part(0)
    arrive(over_z)
    id_half[...] = id_mid[...] + jnp.sum(id_z[...], axis=0)
    ids_copy = send(id_half, id_sib, sibling)
    raw_own.wait_recv()
    meta_copy.wait_recv()
    turned[NX] = sib_raw[0].T
    ids_copy.wait_recv()
    id_full[x] = id_half[...] + id_sib[...]
    ids_x = [send(id_full.at[x], id_full.at[x], on_x(o)) for o in (2, 1, 3)]
    finish_part(1)
    finish_part(2)

    arrive(ids_x)
    table = jnp.concatenate([id_full[i, 0:ZHI, :] for i in range(NX)], axis=0)
    table = table.astype(F32).astype(BF16)
    row = iota((K2 // 2, 1), 0)
    tb = lax.rem(b + lax.div(row, groups_here), NR)
    group_of = c * (K2 // 2) + tb * groups_here + lax.rem(row, groups_here)
    second = jnp.zeros((K2 // 2, width), F32)
    for known, held in ((meta[...], points[...]), (sib_meta[...], sib_raw[0])):
        known = known.astype(I32)
        values = dot(table, one_hot(iota((slot_count, n_points), 0), known[1:2]))
        chosen = iota((NX * ZHI, n_points), 0) == known[0:1]
        groups = jnp.sum(jnp.where(chosen, values, 0.0), axis=0, keepdims=True).astype(I32)
        second = second + dot(one_hot(group_of, groups), held)
    for q in range(NX):
        halves[lax.rem(q - x + NX, NX)] = second[:, q * quarter:(q + 1) * quarter]
    second_x = [send(halves.at[o], land_halves.at[o - 1], on_x(o)) for o in (2, 1, 3)]
    finish_part(3)

    over_b = []

    def finish_a(k):
        total = sums[k, 0]
        for o in range(1, NR):
            over_a[k][o].wait_recv()
            total = total + land_a[k, o - 1]
        mid[:, k * 8:(k + 1) * 8, :] = total.reshape(NR, 8, wide)

    def start_b(first_row):
        part = pl.ds(first_row, 16)
        for o in FAR:
            over_b.append(send(mid.at[o, part], land_b.at[o - 1, part], on_b(o)))

    finish_a(0)
    finish_a(1)
    start_b(0)
    arrive(second_x)
    raw_x = {o: send(points, raw.at[o - 1], on_x(o)) for o in (1, 3)}
    second = halves[0]
    for o in range(1, NX):
        second = second + land_halves[o - 1]
    spread[...] = second.reshape(spread.shape)
    second_b = [send(spread.at[o], land_spread.at[o - 1], on_b(o)) for o in FAR]
    finish_a(2)
    finish_a(3)
    start_b(16)
    arrive(second_b)
    second = spread[0]
    for o in range(1, NR):
        second = second + land_spread[o - 1]
    over_second[a] = second
    second_a = [send(over_second.at[a], over_second.at[a], on_a(o)) for o in FAR]
    arrive(over_b)
    total = mid[0]
    for o in range(1, NR):
        total = total + land_b[o - 1]
    quarters = [total[i * R1:(i + 1) * R1] for i in range(2 * PARTS)]

    def normalize(v):
        return v * lax.rsqrt(jnp.mean(v * v, axis=1, keepdims=True) + 1e-06)

    fetches[1].wait()
    first = jnp.concatenate(quarters, axis=1)
    first = normalize(normalize(first) + old_first[...].astype(F32))
    first_out[...] = first.astype(BF16)
    cents_b[b] = jnp.concatenate(
        [first[:, q * quarter:(q + 1) * quarter] for q in range(4)], axis=0
    ).astype(BF16)
    gather_b = [send(cents_b.at[b], cents_b.at[b], on_b(o)) for o in FAR]

    arrive(second_a)
    second = over_second[0]
    for o in range(1, NR):
        second = second + over_second[o]
    compact[x, b] = second
    seconds_b = [send(compact.at[x, b], compact.at[x, b], on_b(o)) for o in FAR]

    part = n_points // 2
    forward_raw = []
    relay = []
    for o, far, start in ((1, 1, 0), (3, -1, part)):
        raw_x[o].wait_recv()
        piece = pl.ds(start, part)
        relay.append(send(raw.at[o - 1, piece], raw.at[1, piece], on_x(far)))
        forward_raw.append(send(raw.at[o - 1], sib_raw.at[o], sibling))
        turned[o] = raw[o - 1].T

    arrive(gather_b)
    per = NR * R1
    row = iota((4 * per, 1), 0)
    source = lax.div(lax.rem(row, per), R1) * 16 + lax.div(row, per) * R1 + lax.rem(row, R1)
    order = one_hot(source, iota((1, 4 * per), 1))
    block = dot(order, cents_b[...].reshape(4 * per, quarter)).astype(BF16)
    for q in range(4):
        cents[a, :, q * quarter:(q + 1) * quarter] = block[q * per:(q + 1) * per]
    gather_a = [send(cents.at[a], cents.at[a], on_a(o)) for o in FAR]

    arrive(seconds_b)
    compact_x = {o: send(compact.at[x], compact.at[x], on_x(o)) for o in (2, 1, 3)}
    forward_second = [send(compact.at[x], sib_compact.at[x], sibling)]

    arrive(relay)
    forward_raw.append(send(raw.at[1], sib_raw.at[2], sibling))
    turned[2] = raw[1].T
    arrive(forward_raw)
    for o in range(1, NX):
        turned[NX + o] = sib_raw[o].T

    arrive(gather_a)

    table = cents[...].reshape(NR * per, width)
    best_copies = []
    own = None
    for g in (2, 6, 1, 3, 5, 7, 4, 0):
        s = jnp.max(dot(table, turned[g]).reshape(-1, 8, n_points), axis=0)
        if g == 0:
            own = s
        else:
            best_tile[g - 1] = s
            target = on_x(-(g % NX), g // NX)
            best_copies.append(send(best_tile.at[g - 1], best_land.at[g - 1], target))

    for o in (1, 3, 2):
        compact_x[o].wait_recv()
        at = lax.rem(x - o + NX, NX)
        forward_second.append(send(compact.at[at], sib_compact.at[at], sibling))
    fetches[2].wait()
    fetches[3].wait()
    arrive(forward_second)
    for i in range(NX):
        mine = compact[i].reshape(K2 // 2, quarter)
        other = sib_compact[i].reshape(K2 // 2, quarter)
        cols = slice(i * quarter, (i + 1) * quarter)
        second_sum[:K2 // 2, cols] = jnp.where(c == 0, mine, other)
        second_sum[K2 // 2:, cols] = jnp.where(c == 0, other, mine)
    second = second_sum[...]
    second_out[...] = normalize(normalize(second) + old_second[...].astype(F32)).astype(BF16)
    pick = (iota((K3, K2), 0) == third_ids[...]).astype(F32)
    third = dot(pick, second, precision=lax.Precision.HIGHEST)
    third_out[...] = normalize(normalize(third) + old_third[...].astype(F32)).astype(BF16)

    arrive(best_copies)
    top = jnp.maximum(own, jnp.max(best_land[...], axis=0))
    best_out[...] = jnp.max(top, axis=0, keepdims=True) * (1.0 / math.sqrt(width))
    for copy in started:
        copy.wait_send()


def body(
    points, owner_block, centroid_slot, old_first, group_second, group_third, old_second, old_third
):
    n_points, width = points.shape
    quarter, step = width // 4, width // PARTS
    wide = step // 2
    slot_count = NR * ZLO * 2 * R1
    vmem = pl.BlockSpec(memory_space=pltpu.VMEM)
    smem = pl.BlockSpec(memory_space=pltpu.SMEM)
    hbm = pl.BlockSpec(memory_space=pltpu.HBM)
    copies = 160
    first, second, third, best = pl.pallas_call(
        kernel,
        out_shape=(
            jax.ShapeDtypeStruct((R1, width), BF16),
            jax.ShapeDtypeStruct((K2, width), BF16),
            jax.ShapeDtypeStruct((K3, width), BF16),
            jax.ShapeDtypeStruct((1, n_points), F32),
        ),
        in_specs=[hbm, vmem, vmem, hbm, smem, vmem, hbm, hbm],
        out_specs=(vmem, vmem, vmem, vmem),
        scratch_shapes=[
            pltpu.VMEM((n_points, width), BF16),
            pltpu.VMEM((R1, width), BF16),
            pltpu.VMEM((K2, width), BF16),
            pltpu.VMEM((K3, width), BF16),
            pltpu.VMEM((PARTS, NX - 1, ROWS, step), BF16),
            pltpu.VMEM((NX - 1, 8, ROWS), F32),
            pltpu.VMEM((PARTS, 2 * NX, ROWS, step), BF16),
            pltpu.VMEM((2 * NX, 8, ROWS), F32),
            pltpu.VMEM((2, 2, NR * NR * 8, NX * ROWS), BF16),
            pltpu.VMEM((NX - 1, n_points, width), BF16),
            pltpu.VMEM((NX, n_points, width), BF16),
            pltpu.VMEM((8, n_points), F32),
            pltpu.VMEM((8, n_points), F32),
            pltpu.VMEM((2 * NX, width, n_points), BF16),
            pltpu.VMEM((8, slot_count), I32),
            pltpu.VMEM((NR - 1, 8, slot_count), I32),
            pltpu.VMEM((8, slot_count), I32),
            pltpu.VMEM((NR - 1, 8, slot_count), I32),
            pltpu.VMEM((8, slot_count), I32),
            pltpu.VMEM((8, slot_count), I32),
            pltpu.VMEM((NX, 8, slot_count), I32),
            pltpu.VMEM((PARTS, NR, NR * 8, wide), F32),
            pltpu.VMEM((PARTS, NR - 1, NR * 8, wide), F32),
            pltpu.VMEM((NR, PARTS * 8, wide), F32),
            pltpu.VMEM((NR - 1, PARTS * 8, wide), F32),
            pltpu.VMEM((NX, K2 // 2, quarter), F32),
            pltpu.VMEM((NX - 1, K2 // 2, quarter), F32),
            pltpu.VMEM((NR, K2 // 2 // NR, quarter), F32),
            pltpu.VMEM((NR - 1, K2 // 2 // NR, quarter), F32),
            pltpu.VMEM((NR, K2 // 2 // NR, quarter), F32),
            pltpu.VMEM((NR, 4 * R1, quarter), BF16),
            pltpu.VMEM((NR, NR * R1, width), BF16),
            pltpu.VMEM((NX, NR, K2 // 2 // NR, quarter), F32),
            pltpu.VMEM((NX, NR, K2 // 2 // NR, quarter), F32),
            pltpu.VMEM((K2, width), F32),
            pltpu.VMEM((2 * NX - 1, 8, n_points), F32),
            pltpu.VMEM((2 * NX - 1, 8, n_points), F32),
            pltpu.SemaphoreType.DMA((4,)),
            pltpu.SemaphoreType.DMA((copies,)),
            pltpu.SemaphoreType.DMA((copies,)),
        ],
        compiler_params=pltpu.CompilerParams(
            collective_id=0, has_side_effects=True, vmem_limit_bytes=32 * 1024 * 1024
        ),
    )(
        points,
        owner_block.reshape(1, n_points),
        centroid_slot.reshape(1, n_points),
        old_first,
        group_second,
        group_third.reshape(1, K2),
        old_second,
        old_third,
    )
    return first, second, third, best.reshape(n_points)


def solution(mesh):
    in_specs = (
        P(("dp", "cent"), None),
        P(("dp", "cent"), None),
        P(("dp", "cent")),
        P(("dp", "cent"), None),
        P(("dp", "cent")),
        P(),
        P(),
        P(),
    )
    out_specs = (P(("dp", "cent"), None), P(), P(), P(("dp", "cent")))
    return jax.shard_map(body, mesh=mesh, in_specs=in_specs, out_specs=out_specs, check_vma=False)
```

```python
import math

import jax
import jax.numpy as jnp
from jax import lax
from jax.experimental import pallas as pl
from jax.experimental.pallas import tpu as pltpu
from jax.sharding import PartitionSpec as P

MESH = pl.DeviceIdType.MESH
F32, BF16, I32 = jnp.float32, jnp.bfloat16, jnp.int32

NX = 4
NR = 8
ZLO = 2
ZHI = NR // ZLO
R1 = 4
K2 = 256
K3 = 16
CAP = 32
PARTS = 4
AHEAD = 2
ROWS = ZHI * CAP


def iota(shape, axis):
    return lax.broadcasted_iota(I32, shape, axis)


def dot(a, b, contract=((1,), (0,)), **kw):
    return lax.dot_general(a, b, (contract, ((), ())), preferred_element_type=F32, **kw)


FAR = (4, 3, 5, 2, 6, 1, 7)


def kernel(
    points_in, owners, slots, old_first_in, ids, third_ids, old_second_in, old_third_in,
    first_out, second_out, third_out, best_out,
    points, old_first, old_second, old_third, packed, packed_keys, rows, keys, hot,
    raw, sib_raw, meta, sib_meta, turned, id_tile, id_y, id_mid, id_z, id_half, id_sib, id_full,
    sums, land_a, mid, land_b, halves, land_halves, spread, land_spread, over_second,
    cents_b, cents, compact, best_tile, best_land,
    local_sem, send_sem, recv_sem,
):
    fetches = [
        pltpu.make_async_copy(src, dst, local_sem.at[n])
        for n, (src, dst) in enumerate((
            (points_in, points), (old_first_in, old_first),
            (old_second_in, old_second), (old_third_in, old_third),
        ))
    ]
    for fetch in fetches:
        fetch.start()

    dp, cent = lax.axis_index("dp"), lax.axis_index("cent")
    c = lax.rem(dp, 2)
    zlo = lax.rem(lax.div(dp, 2), ZLO)
    y = lax.div(dp, 2 * ZLO)
    x = lax.div(cent, ZHI)
    z = lax.rem(cent, ZHI) * ZLO + zlo
    a = y + c * (z - y)
    b = z + c * (y - z)
    slot_count = NR * ZLO * 2 * R1
    n_points, width = points.shape
    quarter = width // 4
    step = width // PARTS
    wide = step // 2
    groups_here = K2 // 2 // NR

    def device(x_, y_, z_, c_):
        return ((y_ * ZLO + lax.rem(z_, ZLO)) * 2 + c_, x_ * ZHI + lax.div(z_, ZLO))

    def on_x(o, core=0):
        return device(lax.rem(x + o + NX, NX), y, z, lax.rem(c + core, 2))

    def on_y(o):
        return device(x, lax.rem(y + o, NR), z, c)

    def on_z(o):
        return device(x, y, lax.rem(z + o, NR), c)

    def on_a(o):
        t = lax.rem(a + o, NR)
        return device(x, y + (1 - c) * (t - y), z + c * (t - z), c)

    def on_b(o):
        t = lax.rem(b + o, NR)
        return device(x, y + c * (t - y), z + (1 - c) * (t - z), c)

    sibling = device(x, y, z, 1 - c)

    barrier = pltpu.get_barrier_semaphore()
    partners = [sibling]
    partners += [on_x(o, core) for o in range(1, NX) for core in range(2)]
    partners += [on_y(o) for o in range(1, NR)]
    partners += [on_z(o) for o in range(1, NR)]
    for partner in partners:
        pl.semaphore_signal(barrier, inc=1, device_id=partner, device_id_type=MESH)

    started = []

    def send(src, dst, target):
        n = len(started)
        copy = pltpu.make_async_remote_copy(
            src_ref=src, dst_ref=dst, send_sem=send_sem.at[n], recv_sem=recv_sem.at[n],
            device_id=target, device_id_type=MESH,
        )
        copy.start()
        started.append(copy)
        return copy

    def arrive(copies):
        for copy in copies:
            copy.wait_recv()

    base = ((y * ZLO + zlo) * 2 + c) * R1
    tile = jnp.zeros(id_tile.shape, I32)
    for r in range(R1):
        here = (iota(id_tile.shape, 0) == lax.div(z, ZLO)) & (iota(id_tile.shape, 1) == base + r)
        tile = tile + jnp.where(here, ids[r], 0)
    id_tile[...] = tile

    owner = owners[...]
    rel = lax.rem(lax.div(owner, ZHI) - x + NX, NX)
    key = lax.rem(owner, ZHI) * slot_count + slots[...]
    choose = (iota((16, n_points), 0) == rel).astype(F32)
    before = (iota((n_points, n_points), 0) < iota((n_points, n_points), 1)).astype(BF16)
    ranks = dot(choose.astype(BF16), before)
    rank = jnp.sum(ranks * choose, axis=0, keepdims=True).astype(I32)
    spot = rel * ROWS + rank
    place = (iota((NX * ROWS, n_points), 0) == spot).astype(F32).astype(BF16)
    which = iota((16, n_points), 0)
    parts = jnp.where(which == 0, lax.div(key, 16), jnp.where(which == 1, lax.rem(key, 16), 1))
    key_rows = dot(parts.astype(F32).astype(BF16), place, ((1,), (1,)))
    key_row = jnp.where(key_rows[2:3] > 0.5, key_rows[0:1] * 16.0 + key_rows[1:2], -1.0)
    for o in range(NX):
        block_keys = jnp.broadcast_to(key_row[:, o * ROWS:(o + 1) * ROWS], (8, ROWS))
        if o == 0:
            keys[0] = block_keys
        else:
            packed_keys[o - 1] = block_keys
    meta[...] = jnp.where(iota(meta.shape, 0) == 0, owner, slots[...]).astype(F32)

    pl.semaphore_wait(barrier, len(partners))

    over_y = [send(id_tile, id_y.at[o - 1], on_y(o)) for o in range(1, NR)]
    keys_x = [send(packed_keys.at[o - 1], keys.at[o], on_x(o)) for o in (2, 1, 3)]
    forward_keys = [send(keys.at[0], keys.at[NX], sibling)]
    fetches[0].wait()
    over_x, forward = {}, {}

    def send_part(k):
        over_x[k] = [send(packed.at[k, o - 1], rows.at[k, o], on_x(o)) for o in (2, 1, 3)]

    for k in range(PARTS):
        cols = slice(k * step, (k + 1) * step)
        for o in (2, 1, 3, 0):
            block = dot(place[o * ROWS:(o + 1) * ROWS], points[:, cols]).astype(BF16)
            if o == 0:
                rows[k, 0] = block
                forward[k] = [send(rows.at[k, 0], rows.at[k, NX], sibling)]
            else:
                packed[k, o - 1] = block
        if k < AHEAD:
            send_part(k)
    meta_copy = send(meta, sib_meta, sibling)
    raw_own = send(points, sib_raw.at[0], sibling)
    turned[0] = points[...].T

    arrive(over_y)
    id_mid[...] = id_tile[...] + jnp.sum(id_y[...], axis=0)
    over_z = [send(id_mid, id_z.at[o - 1], on_z(o)) for o in range(1, NR)]

    def one_hot(of, values):
        return (of == values).astype(F32).astype(BF16)

    count = NR * NR * 8
    lanes = NX * ROWS
    row = iota((count, 1), 0)
    ta = lax.rem(a + lax.div(row, NR * 8), NR)
    tb = lax.rem(b + lax.rem(lax.div(row, 8), NR), NR)
    ty = ta + c * (tb - ta)
    tz = tb + c * (ta - tb)
    within = lax.rem(row, 8)
    slot = ((ty * ZLO + lax.rem(tz, ZLO)) * 2 + c) * R1 + lax.rem(within, R1)
    key_of = lax.div(tz, ZLO) * slot_count + slot
    side_keys = (jnp.where(within < R1, key_of, -2), jnp.where(within >= R1, key_of, -2))

    def fill_hot(core):
        span = range(core * NX, (core + 1) * NX)
        key_row = jnp.concatenate([keys[i, 0:1, :] for i in span], axis=1).astype(I32)
        for side in range(2):
            hot[core, side] = one_hot(side_keys[side], key_row)

    def sum_part(k, core):
        held = rows[k, core * NX:(core + 1) * NX].reshape(lanes, step)
        part = dot(hot[core, 0], held[:, :wide]) + dot(hot[core, 1], held[:, wide:])
        return part.reshape(NR, NR * 8, wide)

    over_a = {}
    part = n_points // 2
    first_piece, last_piece = pl.ds(0, part), pl.ds(part, part)

    def send_raw_pieces():
        one, other = {}, {}
        for pieces in ((first_piece, last_piece), (last_piece, first_piece)):
            for o, piece in zip((1, 3), pieces):
                into = one if o not in one else other
                into[o] = send(points.at[piece], raw.at[o - 1, piece], on_x(o))
        return {o: (one[o], other[o]) for o in (1, 3)}


    def finish_part(k):
        arrive(over_x[k])
        if k + AHEAD < PARTS:
            send_part(k + AHEAD)
        span = pl.ds(1, NX - 1)
        onward = pl.ds(NX + 1, NX - 1)
        forward[k].append(send(rows.at[k, span], rows.at[k, onward], sibling))
        sums[k] = sum_part(k, 0)
        arrive(forward[k])
        sums[k] = sums[k] + sum_part(k, 1)
        over_a[k] = {o: send(sums.at[k, o], land_a.at[k, o - 1], on_a(o)) for o in FAR}

    arrive(keys_x)
    for o in range(1, NX):
        forward_keys.append(send(keys.at[o], keys.at[NX + o], sibling))
    fill_hot(0)
    arrive(forward_keys)
    fill_hot(1)
    finish_part(0)
    arrive(over_z)
    id_half[...] = id_mid[...] + jnp.sum(id_z[...], axis=0)
    ids_copy = send(id_half, id_sib, sibling)
    raw_own.wait_recv()
    meta_copy.wait_recv()
    turned[NX] = sib_raw[0].T
    ids_copy.wait_recv()
    id_full[x] = id_half[...] + id_sib[...]
    ids_x = [send(id_full.at[x], id_full.at[x], on_x(o)) for o in (2, 1, 3)]
    finish_part(1)
    finish_part(2)

    arrive(ids_x)
    table = jnp.concatenate([id_full[i, 0:ZHI, :] for i in range(NX)], axis=0)
    table = table.astype(F32).astype(BF16)
    row = iota((K2 // 2, 1), 0)
    tb = lax.rem(b + lax.div(row, groups_here), NR)
    group_of = c * (K2 // 2) + tb * groups_here + lax.rem(row, groups_here)
    second = jnp.zeros((K2 // 2, width), F32)
    for known, held in ((meta[...], points[...]), (sib_meta[...], sib_raw[0])):
        known = known.astype(I32)
        values = dot(table, one_hot(iota((slot_count, n_points), 0), known[1:2]))
        chosen = iota((NX * ZHI, n_points), 0) == known[0:1]
        groups = jnp.sum(jnp.where(chosen, values, 0.0), axis=0, keepdims=True).astype(I32)
        second = second + dot(one_hot(group_of, groups), held)
    for q in range(NX):
        halves[lax.rem(q - x + NX, NX)] = second[:, q * quarter:(q + 1) * quarter]
    second_x = [send(halves.at[o], land_halves.at[o - 1], on_x(o)) for o in (2, 1, 3)]
    finish_part(3)
    raw_x = send_raw_pieces()

    over_b = []

    def finish_a(k):
        total = sums[k, 0]
        for o in range(1, NR):
            over_a[k][o].wait_recv()
            total = total + land_a[k, o - 1]
        mid[:, k * 8:(k + 1) * 8, :] = total.reshape(NR, 8, wide)

    def start_b(first_row):
        part = pl.ds(first_row, 16)
        for o in FAR:
            over_b.append(send(mid.at[o, part], land_b.at[o - 1, part], on_b(o)))

    finish_a(0)
    finish_a(1)
    start_b(0)
    arrive(second_x)
    second = halves[0]
    for o in range(1, NX):
        second = second + land_halves[o - 1]
    spread[...] = second.reshape(spread.shape)
    second_b = [send(spread.at[o], land_spread.at[o - 1], on_b(o)) for o in FAR]
    finish_a(2)
    finish_a(3)
    start_b(16)
    forward_raw = []
    relay = []
    for o, far, piece in ((1, 1, first_piece), (3, -1, last_piece)):
        raw_x[o][0].wait_recv()
        relay.append(send(raw.at[o - 1, piece], raw.at[1, piece], on_x(far)))
    arrive(second_b)
    second = spread[0]
    for o in range(1, NR):
        second = second + land_spread[o - 1]
    over_second[a] = second
    second_a = [send(over_second.at[a], over_second.at[a], on_a(o)) for o in FAR]
    arrive(over_b)
    total = mid[0]
    for o in range(1, NR):
        total = total + land_b[o - 1]
    quarters = [total[i * R1:(i + 1) * R1] for i in range(2 * PARTS)]

    def normalize(v):
        return v * lax.rsqrt(jnp.mean(v * v, axis=1, keepdims=True) + 1e-06)

    fetches[1].wait()
    first = jnp.concatenate(quarters, axis=1)
    first = normalize(normalize(first) + old_first[...].astype(F32))
    first_out[...] = first.astype(BF16)
    cents_b[b] = jnp.concatenate(
        [first[:, q * quarter:(q + 1) * quarter] for q in range(4)], axis=0
    ).astype(BF16)
    gather_b = [send(cents_b.at[b], cents_b.at[b], on_b(o)) for o in FAR]

    arrive(second_a)
    second = over_second[0]
    for o in range(1, NR):
        second = second + over_second[o]
    compact[c, x, b] = second
    seconds_b = [send(compact.at[c, x, b], compact.at[c, x, b], on_b(o)) for o in FAR]

    for o in (1, 3):
        raw_x[o][1].wait_recv()
        forward_raw.append(send(raw.at[o - 1], sib_raw.at[o], sibling))
        turned[o] = raw[o - 1].T

    arrive(gather_b)
    per = NR * R1
    row = iota((4 * per, 1), 0)
    source = lax.div(lax.rem(row, per), R1) * 16 + lax.div(row, per) * R1 + lax.rem(row, R1)
    order = one_hot(source, iota((1, 4 * per), 1))
    block = dot(order, cents_b[...].reshape(4 * per, quarter)).astype(BF16)
    for q in range(4):
        cents[a, :, q * quarter:(q + 1) * quarter] = block[q * per:(q + 1) * per]
    gather_a = [send(cents.at[a], cents.at[a], on_a(o)) for o in FAR]

    arrive(seconds_b)
    compact_x = {o: send(compact.at[c, x], compact.at[c, x], on_x(o)) for o in (2, 1, 3)}
    forward_second = [send(compact.at[c, x], compact.at[c, x], sibling)]

    arrive(relay)
    forward_raw.append(send(raw.at[1], sib_raw.at[2], sibling))
    turned[2] = raw[1].T
    arrive(forward_raw)
    for o in range(1, NX):
        turned[NX + o] = sib_raw[o].T

    arrive(gather_a)

    table = cents[...].reshape(NR * per, width)
    best_copies = []
    own = None
    for g in (2, 6, 1, 3, 5, 7, 4, 0):
        s = jnp.max(dot(table, turned[g]).reshape(-1, 8, n_points), axis=0)
        if g == 0:
            own = s
        else:
            best_tile[g - 1] = s
            target = on_x(-(g % NX), g // NX)
            best_copies.append(send(best_tile.at[g - 1], best_land.at[g - 1], target))

    for o in (1, 3, 2):
        compact_x[o].wait_recv()
        at = lax.rem(x - o + NX, NX)
        forward_second.append(send(compact.at[c, at], compact.at[c, at], sibling))
    fetches[2].wait()
    fetches[3].wait()
    arrive(forward_second)
    third = jnp.zeros((K3, width), F32)
    for core in range(2):
        here = slice(core * (K2 // 2), (core + 1) * (K2 // 2))
        second = jnp.concatenate(
            [compact[core, i].reshape(K2 // 2, quarter) for i in range(NX)], axis=1
        )
        pick = one_hot(iota((K3, K2 // 2), 0), third_ids[:, here])
        left = second
        for _ in range(3):
            piece = left.astype(BF16)
            third = third + dot(pick, piece)
            left = left - piece.astype(F32)
        updated = normalize(normalize(second) + old_second[here, :].astype(F32))
        second_out[here, :] = updated.astype(BF16)
    third_out[...] = normalize(normalize(third) + old_third[...].astype(F32)).astype(BF16)

    arrive(best_copies)
    top = jnp.maximum(own, jnp.max(best_land[...], axis=0))
    best_out[...] = jnp.max(top, axis=0, keepdims=True) * (1.0 / math.sqrt(width))
    for copy in started:
        copy.wait_send()


def body(
    points, owner_block, centroid_slot, old_first, group_second, group_third, old_second, old_third
):
    n_points, width = points.shape
    quarter, step = width // 4, width // PARTS
    wide = step // 2
    slot_count = NR * ZLO * 2 * R1
    vmem = pl.BlockSpec(memory_space=pltpu.VMEM)
    smem = pl.BlockSpec(memory_space=pltpu.SMEM)
    hbm = pl.BlockSpec(memory_space=pltpu.HBM)
    copies = 160
    first, second, third, best = pl.pallas_call(
        kernel,
        out_shape=(
            jax.ShapeDtypeStruct((R1, width), BF16),
            jax.ShapeDtypeStruct((K2, width), BF16),
            jax.ShapeDtypeStruct((K3, width), BF16),
            jax.ShapeDtypeStruct((1, n_points), F32),
        ),
        in_specs=[hbm, vmem, vmem, hbm, smem, vmem, hbm, hbm],
        out_specs=(vmem, vmem, vmem, vmem),
        scratch_shapes=[
            pltpu.VMEM((n_points, width), BF16),
            pltpu.VMEM((R1, width), BF16),
            pltpu.VMEM((K2, width), BF16),
            pltpu.VMEM((K3, width), BF16),
            pltpu.VMEM((PARTS, NX - 1, ROWS, step), BF16),
            pltpu.VMEM((NX - 1, 8, ROWS), F32),
            pltpu.VMEM((PARTS, 2 * NX, ROWS, step), BF16),
            pltpu.VMEM((2 * NX, 8, ROWS), F32),
            pltpu.VMEM((2, 2, NR * NR * 8, NX * ROWS), BF16),
            pltpu.VMEM((NX - 1, n_points, width), BF16),
            pltpu.VMEM((NX, n_points, width), BF16),
            pltpu.VMEM((8, n_points), F32),
            pltpu.VMEM((8, n_points), F32),
            pltpu.VMEM((2 * NX, width, n_points), BF16),
            pltpu.VMEM((8, slot_count), I32),
            pltpu.VMEM((NR - 1, 8, slot_count), I32),
            pltpu.VMEM((8, slot_count), I32),
            pltpu.VMEM((NR - 1, 8, slot_count), I32),
            pltpu.VMEM((8, slot_count), I32),
            pltpu.VMEM((8, slot_count), I32),
            pltpu.VMEM((NX, 8, slot_count), I32),
            pltpu.VMEM((PARTS, NR, NR * 8, wide), F32),
            pltpu.VMEM((PARTS, NR - 1, NR * 8, wide), F32),
            pltpu.VMEM((NR, PARTS * 8, wide), F32),
            pltpu.VMEM((NR - 1, PARTS * 8, wide), F32),
            pltpu.VMEM((NX, K2 // 2, quarter), F32),
            pltpu.VMEM((NX - 1, K2 // 2, quarter), F32),
            pltpu.VMEM((NR, K2 // 2 // NR, quarter), F32),
            pltpu.VMEM((NR - 1, K2 // 2 // NR, quarter), F32),
            pltpu.VMEM((NR, K2 // 2 // NR, quarter), F32),
            pltpu.VMEM((NR, 4 * R1, quarter), BF16),
            pltpu.VMEM((NR, NR * R1, width), BF16),
            pltpu.VMEM((2, NX, NR, K2 // 2 // NR, quarter), F32),
            pltpu.VMEM((2 * NX - 1, 8, n_points), F32),
            pltpu.VMEM((2 * NX - 1, 8, n_points), F32),
            pltpu.SemaphoreType.DMA((4,)),
            pltpu.SemaphoreType.DMA((copies,)),
            pltpu.SemaphoreType.DMA((copies,)),
        ],
        compiler_params=pltpu.CompilerParams(
            collective_id=0, has_side_effects=True, vmem_limit_bytes=850 * 65536
        ),
    )(
        points,
        owner_block.reshape(1, n_points),
        centroid_slot.reshape(1, n_points),
        old_first,
        group_second,
        group_third.reshape(1, K2),
        old_second,
        old_third,
    )
    return first, second, third, best.reshape(n_points)


def solution(mesh):
    in_specs = (
        P(("dp", "cent"), None),
        P(("dp", "cent"), None),
        P(("dp", "cent")),
        P(("dp", "cent"), None),
        P(("dp", "cent")),
        P(),
        P(),
        P(),
    )
    out_specs = (P(("dp", "cent"), None), P(), P(), P(("dp", "cent")))
    return jax.shard_map(body, mesh=mesh, in_specs=in_specs, out_specs=out_specs, check_vma=False)
```

```python
import math

import jax
import jax.numpy as jnp
from jax import lax
from jax.experimental import pallas as pl
from jax.experimental.pallas import tpu as pltpu
from jax.sharding import PartitionSpec as P

MESH = pl.DeviceIdType.MESH
F32, BF16, I32 = jnp.float32, jnp.bfloat16, jnp.int32

NX = 4
NR = 8
ZLO = 2
ZHI = NR // ZLO
R1 = 4
K2 = 256
K3 = 16
CAP = 32
PARTS = 4
AHEAD = 2
ROWS = ZHI * CAP


def iota(shape, axis):
    return lax.broadcasted_iota(I32, shape, axis)


def dot(a, b, contract=((1,), (0,)), **kw):
    return lax.dot_general(a, b, (contract, ((), ())), preferred_element_type=F32, **kw)


FAR = (4, 3, 5, 2, 6, 1, 7)


def kernel(
    points_in, owners, slots, old_first_in, ids, third_ids, old_second_in, old_third_in,
    first_out, second_out, third_out, best_out,
    points, old_first, old_second, old_third, packed, packed_keys, rows, keys, hot,
    raw, sib_raw, meta, sib_meta, turned, id_tile, id_y, id_mid, id_z, id_half, id_sib, id_full,
    sums, land_a, mid, land_b, halves, land_halves, spread, land_spread, over_second,
    cents_b, cents, compact, best_tile, best_land,
    local_sem, send_sem, recv_sem,
):
    fetches = [
        pltpu.make_async_copy(src, dst, local_sem.at[n])
        for n, (src, dst) in enumerate((
            (points_in, points), (old_first_in, old_first),
            (old_second_in, old_second), (old_third_in, old_third),
        ))
    ]
    for fetch in fetches:
        fetch.start()

    dp, cent = lax.axis_index("dp"), lax.axis_index("cent")
    c = lax.rem(dp, 2)
    zlo = lax.rem(lax.div(dp, 2), ZLO)
    y = lax.div(dp, 2 * ZLO)
    x = lax.div(cent, ZHI)
    z = lax.rem(cent, ZHI) * ZLO + zlo
    a = y + c * (z - y)
    b = z + c * (y - z)
    slot_count = NR * ZLO * 2 * R1
    n_points, width = points.shape
    quarter = width // 4
    step = width // PARTS
    wide = step // 2
    groups_here = K2 // 2 // NR

    def device(x_, y_, z_, c_):
        return ((y_ * ZLO + lax.rem(z_, ZLO)) * 2 + c_, x_ * ZHI + lax.div(z_, ZLO))

    def on_x(o, core=0):
        return device(lax.rem(x + o + NX, NX), y, z, lax.rem(c + core, 2))

    def on_y(o):
        return device(x, lax.rem(y + o, NR), z, c)

    def on_z(o):
        return device(x, y, lax.rem(z + o, NR), c)

    def on_a(o):
        t = lax.rem(a + o, NR)
        return device(x, y + (1 - c) * (t - y), z + c * (t - z), c)

    def on_b(o):
        t = lax.rem(b + o, NR)
        return device(x, y + c * (t - y), z + (1 - c) * (t - z), c)

    sibling = device(x, y, z, 1 - c)

    barrier = pltpu.get_barrier_semaphore()
    partners = [sibling]
    partners += [on_x(o, core) for o in range(1, NX) for core in range(2)]
    partners += [on_y(o) for o in range(1, NR)]
    partners += [on_z(o) for o in range(1, NR)]
    for partner in partners:
        pl.semaphore_signal(barrier, inc=1, device_id=partner, device_id_type=MESH)

    started = []

    def send(src, dst, target):
        n = len(started)
        copy = pltpu.make_async_remote_copy(
            src_ref=src, dst_ref=dst, send_sem=send_sem.at[n], recv_sem=recv_sem.at[n],
            device_id=target, device_id_type=MESH,
        )
        copy.start()
        started.append(copy)
        return copy

    def arrive(copies):
        for copy in copies:
            copy.wait_recv()

    base = ((y * ZLO + zlo) * 2 + c) * R1
    tile = jnp.zeros(id_tile.shape, I32)
    for r in range(R1):
        here = (iota(id_tile.shape, 0) == lax.div(z, ZLO)) & (iota(id_tile.shape, 1) == base + r)
        tile = tile + jnp.where(here, ids[r], 0)
    id_tile[...] = tile

    owner = owners[...]
    rel = lax.rem(lax.div(owner, ZHI) - x + NX, NX)
    key = lax.rem(owner, ZHI) * slot_count + slots[...]
    choose = (iota((16, n_points), 0) == rel).astype(F32)
    before = (iota((n_points, n_points), 0) < iota((n_points, n_points), 1)).astype(BF16)
    ranks = dot(choose.astype(BF16), before)
    rank = jnp.sum(ranks * choose, axis=0, keepdims=True).astype(I32)
    spot = rel * ROWS + rank
    place = (iota((NX * ROWS, n_points), 0) == spot).astype(F32).astype(BF16)
    which = iota((16, n_points), 0)
    parts = jnp.where(which == 0, lax.div(key, 16), jnp.where(which == 1, lax.rem(key, 16), 1))
    key_rows = dot(parts.astype(F32).astype(BF16), place, ((1,), (1,)))
    key_row = jnp.where(key_rows[2:3] > 0.5, key_rows[0:1] * 16.0 + key_rows[1:2], -1.0)
    for o in range(NX):
        block_keys = jnp.broadcast_to(key_row[:, o * ROWS:(o + 1) * ROWS], (8, ROWS))
        if o == 0:
            keys[0] = block_keys
        else:
            packed_keys[o - 1] = block_keys
    meta[...] = jnp.where(iota(meta.shape, 0) == 0, owner, slots[...]).astype(F32)

    pl.semaphore_wait(barrier, len(partners))

    over_y = [send(id_tile, id_y.at[o - 1], on_y(o)) for o in range(1, NR)]
    keys_x = [send(packed_keys.at[o - 1], keys.at[o], on_x(o)) for o in (2, 1, 3)]
    forward_keys = [send(keys.at[0], keys.at[NX], sibling)]
    fetches[0].wait()
    over_x, forward = {}, {}

    def send_part(k):
        over_x[k] = [send(packed.at[k, o - 1], rows.at[k, o], on_x(o)) for o in (2, 1, 3)]

    for k in range(PARTS):
        cols = slice(k * step, (k + 1) * step)
        for o in (2, 1, 3, 0):
            block = dot(place[o * ROWS:(o + 1) * ROWS], points[:, cols]).astype(BF16)
            if o == 0:
                rows[k, 0] = block
                forward[k] = [send(rows.at[k, 0], rows.at[k, NX], sibling)]
            else:
                packed[k, o - 1] = block
        if k < AHEAD:
            send_part(k)
    meta_copy = send(meta, sib_meta, sibling)
    raw_own = send(points, sib_raw.at[0], sibling)
    turned[0] = points[...].T

    arrive(over_y)
    id_mid[...] = id_tile[...] + jnp.sum(id_y[...], axis=0)
    over_z = [send(id_mid, id_z.at[o - 1], on_z(o)) for o in range(1, NR)]

    def one_hot(of, values):
        return (of == values).astype(F32).astype(BF16)

    count = NR * NR * 8
    lanes = NX * ROWS
    row = iota((count, 1), 0)
    ta = lax.rem(a + lax.div(row, NR * 8), NR)
    tb = lax.rem(b + lax.rem(lax.div(row, 8), NR), NR)
    ty = ta + c * (tb - ta)
    tz = tb + c * (ta - tb)
    within = lax.rem(row, 8)
    slot = ((ty * ZLO + lax.rem(tz, ZLO)) * 2 + c) * R1 + lax.rem(within, R1)
    key_of = lax.div(tz, ZLO) * slot_count + slot
    side_keys = (jnp.where(within < R1, key_of, -2), jnp.where(within >= R1, key_of, -2))

    def fill_hot(core):
        span = range(core * NX, (core + 1) * NX)
        key_row = jnp.concatenate([keys[i, 0:1, :] for i in span], axis=1).astype(I32)
        for side in range(2):
            hot[core, side] = one_hot(side_keys[side], key_row)

    def sum_part(k, core):
        held = rows[k, core * NX:(core + 1) * NX].reshape(lanes, step)
        part = dot(hot[core, 0], held[:, :wide]) + dot(hot[core, 1], held[:, wide:])
        return part.reshape(NR, NR * 8, wide)

    over_a = {}
    part = n_points // 2
    first_piece, last_piece = pl.ds(0, part), pl.ds(part, part)

    def send_raw_pieces():
        one, other = {}, {}
        for pieces in ((first_piece, last_piece), (last_piece, first_piece)):
            for o, piece in zip((1, 3), pieces):
                into = one if o not in one else other
                into[o] = send(points.at[piece], raw.at[o - 1, piece], on_x(o))
        return {o: (one[o], other[o]) for o in (1, 3)}


    def finish_part(k):
        arrive(over_x[k])
        if k + AHEAD < PARTS:
            send_part(k + AHEAD)
        span = pl.ds(1, NX - 1)
        onward = pl.ds(NX + 1, NX - 1)
        forward[k].append(send(rows.at[k, span], rows.at[k, onward], sibling))
        sums[k] = sum_part(k, 0)
        arrive(forward[k])
        sums[k] = sums[k] + sum_part(k, 1)
        over_a[k] = {o: send(sums.at[k, o], land_a.at[k, o - 1], on_a(o)) for o in FAR}

    arrive(keys_x)
    for o in range(1, NX):
        forward_keys.append(send(keys.at[o], keys.at[NX + o], sibling))
    fill_hot(0)
    arrive(forward_keys)
    fill_hot(1)
    finish_part(0)
    arrive(over_z)
    id_half[...] = id_mid[...] + jnp.sum(id_z[...], axis=0)
    ids_copy = send(id_half, id_sib, sibling)
    raw_own.wait_recv()
    meta_copy.wait_recv()
    turned[NX] = sib_raw[0].T
    ids_copy.wait_recv()
    id_full[x] = id_half[...] + id_sib[...]
    ids_x = [send(id_full.at[x], id_full.at[x], on_x(o)) for o in (2, 1, 3)]
    finish_part(1)
    finish_part(2)

    arrive(ids_x)
    table = jnp.concatenate([id_full[i, 0:ZHI, :] for i in range(NX)], axis=0)
    table = table.astype(F32).astype(BF16)
    row = iota((K2 // 2, 1), 0)
    tb = lax.rem(b + lax.div(row, groups_here), NR)
    group_of = c * (K2 // 2) + tb * groups_here + lax.rem(row, groups_here)
    second = jnp.zeros((K2 // 2, width), F32)
    for known, held in ((meta[...], points[...]), (sib_meta[...], sib_raw[0])):
        known = known.astype(I32)
        values = dot(table, one_hot(iota((slot_count, n_points), 0), known[1:2]))
        chosen = iota((NX * ZHI, n_points), 0) == known[0:1]
        groups = jnp.sum(jnp.where(chosen, values, 0.0), axis=0, keepdims=True).astype(I32)
        second = second + dot(one_hot(group_of, groups), held)
    for q in range(NX):
        halves[lax.rem(q - x + NX, NX)] = second[:, q * quarter:(q + 1) * quarter]
    second_x = [send(halves.at[o], land_halves.at[o - 1], on_x(o)) for o in (2, 1, 3)]
    finish_part(3)
    raw_x = send_raw_pieces()

    over_b = []

    def finish_a(k):
        total = sums[k, 0]
        for o in range(1, NR):
            over_a[k][o].wait_recv()
            total = total + land_a[k, o - 1]
        mid[:, k * 8:(k + 1) * 8, :] = total.reshape(NR, 8, wide)

    def start_b(first_row):
        part = pl.ds(first_row, 16)
        for o in FAR:
            over_b.append(send(mid.at[o, part], land_b.at[o - 1, part], on_b(o)))

    finish_a(0)
    finish_a(1)
    start_b(0)
    arrive(second_x)
    second = halves[0]
    for o in range(1, NX):
        second = second + land_halves[o - 1]
    spread[...] = second.reshape(spread.shape)
    second_b = [send(spread.at[o], land_spread.at[o - 1], on_b(o)) for o in FAR]
    finish_a(2)
    finish_a(3)
    start_b(16)
    forward_raw = []
    relay = []
    for o, far, piece in ((1, 1, first_piece), (3, -1, last_piece)):
        raw_x[o][0].wait_recv()
        relay.append(send(raw.at[o - 1, piece], raw.at[1, piece], on_x(far)))
    arrive(second_b)
    second = spread[0]
    for o in range(1, NR):
        second = second + land_spread[o - 1]
    over_second[a] = second
    second_a = [send(over_second.at[a], over_second.at[a], on_a(o)) for o in FAR]
    arrive(over_b)
    total = mid[0]
    for o in range(1, NR):
        total = total + land_b[o - 1]
    quarters = [total[i * R1:(i + 1) * R1] for i in range(2 * PARTS)]

    def normalize(v):
        return v * lax.rsqrt(jnp.mean(v * v, axis=1, keepdims=True) + 1e-06)

    fetches[1].wait()
    first = jnp.concatenate(quarters, axis=1)
    first = normalize(normalize(first) + old_first[...].astype(F32))
    first_out[...] = first.astype(BF16)
    cents_b[b] = jnp.concatenate(
        [first[:, q * quarter:(q + 1) * quarter] for q in range(4)], axis=0
    ).astype(BF16)
    gather_b = [send(cents_b.at[b], cents_b.at[b], on_b(o)) for o in FAR]

    arrive(second_a)
    second = over_second[0]
    for o in range(1, NR):
        second = second + over_second[o]
    compact[c, x, b] = second
    seconds_b = [send(compact.at[c, x, b], compact.at[c, x, b], on_b(o)) for o in FAR]

    for o in (1, 3):
        raw_x[o][1].wait_recv()
        forward_raw.append(send(raw.at[o - 1], sib_raw.at[o], sibling))
        turned[o] = raw[o - 1].T

    arrive(gather_b)
    per = NR * R1
    row = iota((4 * per, 1), 0)
    source = lax.div(lax.rem(row, per), R1) * 16 + lax.div(row, per) * R1 + lax.rem(row, R1)
    order = one_hot(source, iota((1, 4 * per), 1))
    block = dot(order, cents_b[...].reshape(4 * per, quarter)).astype(BF16)
    for q in range(4):
        cents[a, :, q * quarter:(q + 1) * quarter] = block[q * per:(q + 1) * per]
    settled = len(started)
    gather_a = [send(cents.at[a], cents.at[a], on_a(o)) for o in FAR]

    arrive(seconds_b)
    compact_x = {o: send(compact.at[c, x], compact.at[c, x], on_x(o)) for o in (2, 1, 3)}
    forward_second = [send(compact.at[c, x], compact.at[c, x], sibling)]

    arrive(relay)
    forward_raw.append(send(raw.at[1], sib_raw.at[2], sibling))
    turned[2] = raw[1].T
    for copy, o in zip(forward_raw, (1, 3)):
        copy.wait_recv()
        turned[NX + o] = sib_raw[o].T

    for copy in started[:settled]:
        copy.wait_send()
    arrive(gather_a)

    table = cents[...].reshape(NR * per, width)
    best_copies = []
    own = None
    for g in (2, 1, 3, 5, 7, 6, 4, 0):
        if g == NX + 2:
            forward_raw[2].wait_recv()
            turned[g] = sib_raw[2].T
        s = jnp.max(dot(table, turned[g]).reshape(-1, 8, n_points), axis=0)
        if g == 0:
            own = s
        else:
            best_tile[g - 1] = s
            target = on_x(-(g % NX), g // NX)
            best_copies.append(send(best_tile.at[g - 1], best_land.at[g - 1], target))

    for o in (1, 3, 2):
        compact_x[o].wait_recv()
        at = lax.rem(x - o + NX, NX)
        forward_second.append(send(compact.at[c, at], compact.at[c, at], sibling))
    fetches[2].wait()
    fetches[3].wait()
    arrive(forward_second)
    third = jnp.zeros((K3, width), F32)
    for core in range(2):
        here = slice(core * (K2 // 2), (core + 1) * (K2 // 2))
        second = jnp.concatenate(
            [compact[core, i].reshape(K2 // 2, quarter) for i in range(NX)], axis=1
        )
        pick = one_hot(iota((K3, K2 // 2), 0), third_ids[:, here])
        left = second
        for _ in range(3):
            piece = left.astype(BF16)
            third = third + dot(pick, piece)
            left = left - piece.astype(F32)
        updated = normalize(normalize(second) + old_second[here, :].astype(F32))
        second_out[here, :] = updated.astype(BF16)
    third_out[...] = normalize(normalize(third) + old_third[...].astype(F32)).astype(BF16)

    arrive(best_copies)
    top = jnp.maximum(own, jnp.max(best_land[...], axis=0))
    best_out[...] = jnp.max(top, axis=0, keepdims=True) * (1.0 / math.sqrt(width))
    for copy in started[settled:]:
        copy.wait_send()


def body(
    points, owner_block, centroid_slot, old_first, group_second, group_third, old_second, old_third
):
    n_points, width = points.shape
    quarter, step = width // 4, width // PARTS
    wide = step // 2
    slot_count = NR * ZLO * 2 * R1
    vmem = pl.BlockSpec(memory_space=pltpu.VMEM)
    smem = pl.BlockSpec(memory_space=pltpu.SMEM)
    hbm = pl.BlockSpec(memory_space=pltpu.HBM)
    copies = 160
    first, second, third, best = pl.pallas_call(
        kernel,
        out_shape=(
            jax.ShapeDtypeStruct((R1, width), BF16),
            jax.ShapeDtypeStruct((K2, width), BF16),
            jax.ShapeDtypeStruct((K3, width), BF16),
            jax.ShapeDtypeStruct((1, n_points), F32),
        ),
        in_specs=[hbm, vmem, vmem, hbm, smem, vmem, hbm, hbm],
        out_specs=(vmem, vmem, vmem, vmem),
        scratch_shapes=[
            pltpu.VMEM((n_points, width), BF16),
            pltpu.VMEM((R1, width), BF16),
            pltpu.VMEM((K2, width), BF16),
            pltpu.VMEM((K3, width), BF16),
            pltpu.VMEM((PARTS, NX - 1, ROWS, step), BF16),
            pltpu.VMEM((NX - 1, 8, ROWS), F32),
            pltpu.VMEM((PARTS, 2 * NX, ROWS, step), BF16),
            pltpu.VMEM((2 * NX, 8, ROWS), F32),
            pltpu.VMEM((2, 2, NR * NR * 8, NX * ROWS), BF16),
            pltpu.VMEM((NX - 1, n_points, width), BF16),
            pltpu.VMEM((NX, n_points, width), BF16),
            pltpu.VMEM((8, n_points), F32),
            pltpu.VMEM((8, n_points), F32),
            pltpu.VMEM((2 * NX, width, n_points), BF16),
            pltpu.VMEM((8, slot_count), I32),
            pltpu.VMEM((NR - 1, 8, slot_count), I32),
            pltpu.VMEM((8, slot_count), I32),
            pltpu.VMEM((NR - 1, 8, slot_count), I32),
            pltpu.VMEM((8, slot_count), I32),
            pltpu.VMEM((8, slot_count), I32),
            pltpu.VMEM((NX, 8, slot_count), I32),
            pltpu.VMEM((PARTS, NR, NR * 8, wide), F32),
            pltpu.VMEM((PARTS, NR - 1, NR * 8, wide), F32),
            pltpu.VMEM((NR, PARTS * 8, wide), F32),
            pltpu.VMEM((NR - 1, PARTS * 8, wide), F32),
            pltpu.VMEM((NX, K2 // 2, quarter), F32),
            pltpu.VMEM((NX - 1, K2 // 2, quarter), F32),
            pltpu.VMEM((NR, K2 // 2 // NR, quarter), F32),
            pltpu.VMEM((NR - 1, K2 // 2 // NR, quarter), F32),
            pltpu.VMEM((NR, K2 // 2 // NR, quarter), F32),
            pltpu.VMEM((NR, 4 * R1, quarter), BF16),
            pltpu.VMEM((NR, NR * R1, width), BF16),
            pltpu.VMEM((2, NX, NR, K2 // 2 // NR, quarter), F32),
            pltpu.VMEM((2 * NX - 1, 8, n_points), F32),
            pltpu.VMEM((2 * NX - 1, 8, n_points), F32),
            pltpu.SemaphoreType.DMA((4,)),
            pltpu.SemaphoreType.DMA((copies,)),
            pltpu.SemaphoreType.DMA((copies,)),
        ],
        compiler_params=pltpu.CompilerParams(
            collective_id=0, has_side_effects=True, vmem_limit_bytes=850 * 65536
        ),
    )(
        points,
        owner_block.reshape(1, n_points),
        centroid_slot.reshape(1, n_points),
        old_first,
        group_second,
        group_third.reshape(1, K2),
        old_second,
        old_third,
    )
    return first, second, third, best.reshape(n_points)


def solution(mesh):
    in_specs = (
        P(("dp", "cent"), None),
        P(("dp", "cent"), None),
        P(("dp", "cent")),
        P(("dp", "cent"), None),
        P(("dp", "cent")),
        P(),
        P(),
        P(),
    )
    out_specs = (P(("dp", "cent"), None), P(), P(), P(("dp", "cent")))
    return jax.shard_map(body, mesh=mesh, in_specs=in_specs, out_specs=out_specs, check_vma=False)
```

```python
import math

import jax
import jax.numpy as jnp
from jax import lax
from jax.experimental import pallas as pl
from jax.experimental.pallas import tpu as pltpu
from jax.sharding import PartitionSpec as P

MESH = pl.DeviceIdType.MESH
F32, BF16, I32 = jnp.float32, jnp.bfloat16, jnp.int32

NX = 4
NR = 8
ZLO = 2
ZHI = NR // ZLO
R1 = 4
K2 = 256
K3 = 16
CAP = 32
PARTS = 4
AHEAD = 3
ROWS = ZHI * CAP


def iota(shape, axis):
    return lax.broadcasted_iota(I32, shape, axis)


def dot(a, b, contract=((1,), (0,)), **kw):
    return lax.dot_general(a, b, (contract, ((), ())), preferred_element_type=F32, **kw)


FAR = (4, 3, 5, 2, 6, 1, 7)


def kernel(
    points_in, owners, slots, old_first_in, ids, third_ids, old_second_in, old_third_in,
    first_out, second_out, third_out, best_out,
    points, old_first, old_second, old_third, packed, packed_keys, rows, keys, hot,
    raw, sib_raw, meta, sib_meta, turned, id_tile, id_y, id_mid, id_z, id_half, id_sib, id_full,
    sums, land_a, mid, land_b, halves, land_halves, spread, land_spread, over_second,
    cents_b, cents, compact, best_tile, best_land,
    local_sem, send_sem, recv_sem,
):
    fetches = [
        pltpu.make_async_copy(src, dst, local_sem.at[n])
        for n, (src, dst) in enumerate((
            (points_in, points), (old_first_in, old_first),
            (old_second_in, old_second), (old_third_in, old_third),
        ))
    ]
    for fetch in fetches:
        fetch.start()

    dp, cent = lax.axis_index("dp"), lax.axis_index("cent")
    c = lax.rem(dp, 2)
    zlo = lax.rem(lax.div(dp, 2), ZLO)
    y = lax.div(dp, 2 * ZLO)
    x = lax.div(cent, ZHI)
    z = lax.rem(cent, ZHI) * ZLO + zlo
    a = y + c * (z - y)
    b = z + c * (y - z)
    slot_count = NR * ZLO * 2 * R1
    n_points, width = points.shape
    quarter = width // 4
    step = width // PARTS
    wide = step // 2
    groups_here = K2 // 2 // NR

    def device(x_, y_, z_, c_):
        return ((y_ * ZLO + lax.rem(z_, ZLO)) * 2 + c_, x_ * ZHI + lax.div(z_, ZLO))

    def on_x(o, core=0):
        return device(lax.rem(x + o + NX, NX), y, z, lax.rem(c + core, 2))

    def on_y(o):
        return device(x, lax.rem(y + o, NR), z, c)

    def on_z(o):
        return device(x, y, lax.rem(z + o, NR), c)

    def on_a(o):
        t = lax.rem(a + o, NR)
        return device(x, y + (1 - c) * (t - y), z + c * (t - z), c)

    def on_b(o):
        t = lax.rem(b + o, NR)
        return device(x, y + c * (t - y), z + (1 - c) * (t - z), c)

    sibling = device(x, y, z, 1 - c)

    barrier = pltpu.get_barrier_semaphore()
    partners = [sibling]
    partners += [on_x(o, core) for o in range(1, NX) for core in range(2)]
    partners += [on_y(o) for o in range(1, NR)]
    partners += [on_z(o) for o in range(1, NR)]
    for partner in partners:
        pl.semaphore_signal(barrier, inc=1, device_id=partner, device_id_type=MESH)

    started = []

    def send(src, dst, target):
        n = len(started)
        copy = pltpu.make_async_remote_copy(
            src_ref=src, dst_ref=dst, send_sem=send_sem.at[n], recv_sem=recv_sem.at[n],
            device_id=target, device_id_type=MESH,
        )
        copy.start()
        started.append(copy)
        return copy

    def arrive(copies):
        for copy in copies:
            copy.wait_recv()

    base = ((y * ZLO + zlo) * 2 + c) * R1
    tile = jnp.zeros(id_tile.shape, I32)
    for r in range(R1):
        here = (iota(id_tile.shape, 0) == lax.div(z, ZLO)) & (iota(id_tile.shape, 1) == base + r)
        tile = tile + jnp.where(here, ids[r], 0)
    id_tile[...] = tile

    owner = owners[...]
    rel = lax.rem(lax.div(owner, ZHI) - x + NX, NX)
    key = lax.rem(owner, ZHI) * slot_count + slots[...]
    choose = (iota((16, n_points), 0) == rel).astype(F32)
    before = (iota((n_points, n_points), 0) < iota((n_points, n_points), 1)).astype(BF16)
    ranks = dot(choose.astype(BF16), before)
    rank = jnp.sum(ranks * choose, axis=0, keepdims=True).astype(I32)
    spot = rel * ROWS + rank
    place = (iota((NX * ROWS, n_points), 0) == spot).astype(F32).astype(BF16)
    which = iota((16, n_points), 0)
    parts = jnp.where(which == 0, lax.div(key, 16), jnp.where(which == 1, lax.rem(key, 16), 1))
    key_rows = dot(parts.astype(F32).astype(BF16), place, ((1,), (1,)))
    key_row = jnp.where(key_rows[2:3] > 0.5, key_rows[0:1] * 16.0 + key_rows[1:2], -1.0)
    for o in range(NX):
        block_keys = jnp.broadcast_to(key_row[:, o * ROWS:(o + 1) * ROWS], (8, ROWS))
        if o == 0:
            keys[0] = block_keys
        else:
            packed_keys[o - 1] = block_keys
    meta[...] = jnp.where(iota(meta.shape, 0) == 0, owner, slots[...]).astype(F32)

    pl.semaphore_wait(barrier, len(partners))

    over_y = [send(id_tile, id_y.at[o - 1], on_y(o)) for o in range(1, NR)]
    keys_x = [send(packed_keys.at[o - 1], keys.at[o], on_x(o)) for o in (2, 1, 3)]
    forward_keys = [send(keys.at[0], keys.at[NX], sibling)]
    fetches[0].wait()
    over_x, forward = {}, {}

    def send_part(k):
        over_x[k] = [send(packed.at[k, o - 1], rows.at[k, o], on_x(o)) for o in (2, 1, 3)]

    for k in range(PARTS):
        cols = slice(k * step, (k + 1) * step)
        for o in (2, 1, 3, 0):
            block = dot(place[o * ROWS:(o + 1) * ROWS], points[:, cols]).astype(BF16)
            if o == 0:
                rows[k, 0] = block
                forward[k] = [send(rows.at[k, 0], rows.at[k, NX], sibling)]
            else:
                packed[k, o - 1] = block
        if k < AHEAD:
            send_part(k)
    meta_copy = send(meta, sib_meta, sibling)
    raw_own = send(points, sib_raw.at[0], sibling)
    turned[0] = points[...].T

    arrive(over_y)
    id_mid[...] = id_tile[...] + jnp.sum(id_y[...], axis=0)
    over_z = [send(id_mid, id_z.at[o - 1], on_z(o)) for o in range(1, NR)]

    def one_hot(of, values):
        return (of == values).astype(F32).astype(BF16)

    count = NR * NR * 8
    lanes = NX * ROWS
    row = iota((count, 1), 0)
    ta = lax.rem(a + lax.div(row, NR * 8), NR)
    tb = lax.rem(b + lax.rem(lax.div(row, 8), NR), NR)
    ty = ta + c * (tb - ta)
    tz = tb + c * (ta - tb)
    within = lax.rem(row, 8)
    slot = ((ty * ZLO + lax.rem(tz, ZLO)) * 2 + c) * R1 + lax.rem(within, R1)
    key_of = lax.div(tz, ZLO) * slot_count + slot
    side_keys = (jnp.where(within < R1, key_of, -2), jnp.where(within >= R1, key_of, -2))

    def fill_hot(core):
        span = range(core * NX, (core + 1) * NX)
        key_row = jnp.concatenate([keys[i, 0:1, :] for i in span], axis=1).astype(I32)
        for side in range(2):
            hot[core, side] = one_hot(side_keys[side], key_row)

    def sum_part(k, core):
        held = rows[k, core * NX:(core + 1) * NX].reshape(lanes, step)
        part = dot(hot[core, 0], held[:, :wide]) + dot(hot[core, 1], held[:, wide:])
        return part.reshape(NR, NR * 8, wide)

    over_a = {}
    part = n_points // 2
    first_piece, last_piece = pl.ds(0, part), pl.ds(part, part)

    def send_raw_pieces():
        one, other = {}, {}
        for pieces in ((first_piece, last_piece), (last_piece, first_piece)):
            for o, piece in zip((1, 3), pieces):
                into = one if o not in one else other
                into[o] = send(points.at[piece], raw.at[o - 1, piece], on_x(o))
        return {o: (one[o], other[o]) for o in (1, 3)}


    def finish_part(k):
        arrive(over_x[k])
        if k + AHEAD < PARTS:
            send_part(k + AHEAD)
        span = pl.ds(1, NX - 1)
        onward = pl.ds(NX + 1, NX - 1)
        forward[k].append(send(rows.at[k, span], rows.at[k, onward], sibling))
        sums[k] = sum_part(k, 0)
        arrive(forward[k])
        sums[k] = sums[k] + sum_part(k, 1)
        over_a[k] = {o: send(sums.at[k, o], land_a.at[k, o - 1], on_a(o)) for o in FAR}

    arrive(keys_x)
    for o in range(1, NX):
        forward_keys.append(send(keys.at[o], keys.at[NX + o], sibling))
    fill_hot(0)
    arrive(forward_keys)
    fill_hot(1)
    finish_part(0)
    arrive(over_z)
    id_half[...] = id_mid[...] + jnp.sum(id_z[...], axis=0)
    ids_copy = send(id_half, id_sib, sibling)
    raw_own.wait_recv()
    meta_copy.wait_recv()
    turned[NX] = sib_raw[0].T
    ids_copy.wait_recv()
    id_full[x] = id_half[...] + id_sib[...]
    ids_x = [send(id_full.at[x], id_full.at[x], on_x(o)) for o in (2, 1, 3)]
    finish_part(1)
    finish_part(2)

    arrive(ids_x)
    table = jnp.concatenate([id_full[i, 0:ZHI, :] for i in range(NX)], axis=0)
    table = table.astype(F32).astype(BF16)
    row = iota((K2 // 2, 1), 0)
    tb = lax.rem(b + lax.div(row, groups_here), NR)
    group_of = c * (K2 // 2) + tb * groups_here + lax.rem(row, groups_here)
    second = jnp.zeros((K2 // 2, width), F32)
    for known, held in ((meta[...], points[...]), (sib_meta[...], sib_raw[0])):
        known = known.astype(I32)
        values = dot(table, one_hot(iota((slot_count, n_points), 0), known[1:2]))
        chosen = iota((NX * ZHI, n_points), 0) == known[0:1]
        groups = jnp.sum(jnp.where(chosen, values, 0.0), axis=0, keepdims=True).astype(I32)
        second = second + dot(one_hot(group_of, groups), held)
    for q in range(NX):
        halves[lax.rem(q - x + NX, NX)] = second[:, q * quarter:(q + 1) * quarter]
    second_x = [send(halves.at[o], land_halves.at[o - 1], on_x(o)) for o in (2, 1, 3)]
    finish_part(3)
    raw_x = send_raw_pieces()

    over_b = []

    def finish_a(k):
        total = sums[k, 0]
        for o in range(1, NR):
            over_a[k][o].wait_recv()
            total = total + land_a[k, o - 1]
        mid[:, k * 8:(k + 1) * 8, :] = total.reshape(NR, 8, wide)

    def start_b(first_row):
        part = pl.ds(first_row, 16)
        for o in FAR:
            over_b.append(send(mid.at[o, part], land_b.at[o - 1, part], on_b(o)))

    finish_a(0)
    finish_a(1)
    start_b(0)
    arrive(second_x)
    second = halves[0]
    for o in range(1, NX):
        second = second + land_halves[o - 1]
    spread[...] = second.reshape(spread.shape)
    second_b = [send(spread.at[o], land_spread.at[o - 1], on_b(o)) for o in FAR]
    finish_a(2)
    finish_a(3)
    start_b(16)
    forward_raw = []
    relay = []
    for o, far, piece in ((1, 1, first_piece), (3, -1, last_piece)):
        raw_x[o][0].wait_recv()
        relay.append(send(raw.at[o - 1, piece], raw.at[1, piece], on_x(far)))
    arrive(second_b)
    second = spread[0]
    for o in range(1, NR):
        second = second + land_spread[o - 1]
    over_second[a] = second
    second_a = [send(over_second.at[a], over_second.at[a], on_a(o)) for o in FAR]
    arrive(over_b)
    total = mid[0]
    for o in range(1, NR):
        total = total + land_b[o - 1]
    quarters = [total[i * R1:(i + 1) * R1] for i in range(2 * PARTS)]

    def normalize(v):
        return v * lax.rsqrt(jnp.mean(v * v, axis=1, keepdims=True) + 1e-06)

    fetches[1].wait()
    first = jnp.concatenate(quarters, axis=1)
    first = normalize(normalize(first) + old_first[...].astype(F32))
    first_out[...] = first.astype(BF16)
    cents_b[b] = jnp.concatenate(
        [first[:, q * quarter:(q + 1) * quarter] for q in range(4)], axis=0
    ).astype(BF16)
    gather_b = [send(cents_b.at[b], cents_b.at[b], on_b(o)) for o in FAR]

    arrive(second_a)
    second = over_second[0]
    for o in range(1, NR):
        second = second + over_second[o]
    compact[c, x, b] = second
    seconds_b = [send(compact.at[c, x, b], compact.at[c, x, b], on_b(o)) for o in FAR]

    for o in (1, 3):
        raw_x[o][1].wait_recv()
        forward_raw.append(send(raw.at[o - 1], sib_raw.at[o], sibling))
        turned[o] = raw[o - 1].T

    arrive(gather_b)
    per = NR * R1
    row = iota((4 * per, 1), 0)
    source = lax.div(lax.rem(row, per), R1) * 16 + lax.div(row, per) * R1 + lax.rem(row, R1)
    order = one_hot(source, iota((1, 4 * per), 1))
    block = dot(order, cents_b[...].reshape(4 * per, quarter)).astype(BF16)
    for q in range(4):
        cents[a, :, q * quarter:(q + 1) * quarter] = block[q * per:(q + 1) * per]
    settled = len(started)
    gather_a = [send(cents.at[a], cents.at[a], on_a(o)) for o in FAR]

    arrive(seconds_b)
    compact_x = {o: send(compact.at[c, x], compact.at[c, x], on_x(o)) for o in (2, 1, 3)}
    forward_second = [send(compact.at[c, x], compact.at[c, x], sibling)]

    arrive(relay)
    forward_raw.append(send(raw.at[1], sib_raw.at[2], sibling))
    turned[2] = raw[1].T
    for copy, o in zip(forward_raw, (1, 3)):
        copy.wait_recv()
        turned[NX + o] = sib_raw[o].T

    for copy in started[:settled]:
        copy.wait_send()
    arrive(gather_a)

    table = cents[...].reshape(NR * per, width)
    best_copies = []
    own = None
    for g in (2, 1, 3, 5, 7, 6, 4, 0):
        if g == NX + 2:
            forward_raw[2].wait_recv()
            turned[g] = sib_raw[2].T
        s = jnp.max(dot(table, turned[g]).reshape(-1, 8, n_points), axis=0)
        if g == 0:
            own = s
        else:
            best_tile[g - 1] = s
            target = on_x(-(g % NX), g // NX)
            best_copies.append(send(best_tile.at[g - 1], best_land.at[g - 1], target))

    for o in (1, 3, 2):
        compact_x[o].wait_recv()
        at = lax.rem(x - o + NX, NX)
        forward_second.append(send(compact.at[c, at], compact.at[c, at], sibling))
    fetches[2].wait()
    fetches[3].wait()
    arrive(forward_second)
    third = jnp.zeros((K3, width), F32)
    for core in range(2):
        here = slice(core * (K2 // 2), (core + 1) * (K2 // 2))
        second = jnp.concatenate(
            [compact[core, i].reshape(K2 // 2, quarter) for i in range(NX)], axis=1
        )
        pick = one_hot(iota((K3, K2 // 2), 0), third_ids[:, here])
        left = second
        for _ in range(3):
            piece = left.astype(BF16)
            third = third + dot(pick, piece)
            left = left - piece.astype(F32)
        updated = normalize(normalize(second) + old_second[here, :].astype(F32))
        second_out[here, :] = updated.astype(BF16)
    third_out[...] = normalize(normalize(third) + old_third[...].astype(F32)).astype(BF16)

    arrive(best_copies)
    top = jnp.maximum(own, jnp.max(best_land[...], axis=0))
    best_out[...] = jnp.max(top, axis=0, keepdims=True) * (1.0 / math.sqrt(width))
    for copy in started[settled:]:
        copy.wait_send()


def body(
    points, owner_block, centroid_slot, old_first, group_second, group_third, old_second, old_third
):
    n_points, width = points.shape
    quarter, step = width // 4, width // PARTS
    wide = step // 2
    slot_count = NR * ZLO * 2 * R1
    vmem = pl.BlockSpec(memory_space=pltpu.VMEM)
    smem = pl.BlockSpec(memory_space=pltpu.SMEM)
    hbm = pl.BlockSpec(memory_space=pltpu.HBM)
    copies = 160
    first, second, third, best = pl.pallas_call(
        kernel,
        out_shape=(
            jax.ShapeDtypeStruct((R1, width), BF16),
            jax.ShapeDtypeStruct((K2, width), BF16),
            jax.ShapeDtypeStruct((K3, width), BF16),
            jax.ShapeDtypeStruct((1, n_points), F32),
        ),
        in_specs=[hbm, vmem, vmem, hbm, smem, vmem, hbm, hbm],
        out_specs=(vmem, vmem, vmem, vmem),
        scratch_shapes=[
            pltpu.VMEM((n_points, width), BF16),
            pltpu.VMEM((R1, width), BF16),
            pltpu.VMEM((K2, width), BF16),
            pltpu.VMEM((K3, width), BF16),
            pltpu.VMEM((PARTS, NX - 1, ROWS, step), BF16),
            pltpu.VMEM((NX - 1, 8, ROWS), F32),
            pltpu.VMEM((PARTS, 2 * NX, ROWS, step), BF16),
            pltpu.VMEM((2 * NX, 8, ROWS), F32),
            pltpu.VMEM((2, 2, NR * NR * 8, NX * ROWS), BF16),
            pltpu.VMEM((NX - 1, n_points, width), BF16),
            pltpu.VMEM((NX, n_points, width), BF16),
            pltpu.VMEM((8, n_points), F32),
            pltpu.VMEM((8, n_points), F32),
            pltpu.VMEM((2 * NX, width, n_points), BF16),
            pltpu.VMEM((8, slot_count), I32),
            pltpu.VMEM((NR - 1, 8, slot_count), I32),
            pltpu.VMEM((8, slot_count), I32),
            pltpu.VMEM((NR - 1, 8, slot_count), I32),
            pltpu.VMEM((8, slot_count), I32),
            pltpu.VMEM((8, slot_count), I32),
            pltpu.VMEM((NX, 8, slot_count), I32),
            pltpu.VMEM((PARTS, NR, NR * 8, wide), F32),
            pltpu.VMEM((PARTS, NR - 1, NR * 8, wide), F32),
            pltpu.VMEM((NR, PARTS * 8, wide), F32),
            pltpu.VMEM((NR - 1, PARTS * 8, wide), F32),
            pltpu.VMEM((NX, K2 // 2, quarter), F32),
            pltpu.VMEM((NX - 1, K2 // 2, quarter), F32),
            pltpu.VMEM((NR, K2 // 2 // NR, quarter), F32),
            pltpu.VMEM((NR - 1, K2 // 2 // NR, quarter), F32),
            pltpu.VMEM((NR, K2 // 2 // NR, quarter), F32),
            pltpu.VMEM((NR, 4 * R1, quarter), BF16),
            pltpu.VMEM((NR, NR * R1, width), BF16),
            pltpu.VMEM((2, NX, NR, K2 // 2 // NR, quarter), F32),
            pltpu.VMEM((2 * NX - 1, 8, n_points), F32),
            pltpu.VMEM((2 * NX - 1, 8, n_points), F32),
            pltpu.SemaphoreType.DMA((4,)),
            pltpu.SemaphoreType.DMA((copies,)),
            pltpu.SemaphoreType.DMA((copies,)),
        ],
        compiler_params=pltpu.CompilerParams(
            collective_id=0, has_side_effects=True, vmem_limit_bytes=850 * 65536
        ),
    )(
        points,
        owner_block.reshape(1, n_points),
        centroid_slot.reshape(1, n_points),
        old_first,
        group_second,
        group_third.reshape(1, K2),
        old_second,
        old_third,
    )
    return first, second, third, best.reshape(n_points)


def solution(mesh):
    in_specs = (
        P(("dp", "cent"), None),
        P(("dp", "cent"), None),
        P(("dp", "cent")),
        P(("dp", "cent"), None),
        P(("dp", "cent")),
        P(),
        P(),
        P(),
    )
    out_specs = (P(("dp", "cent"), None), P(), P(), P(("dp", "cent")))
    return jax.shard_map(body, mesh=mesh, in_specs=in_specs, out_specs=out_specs, check_vma=False)
```
